32 devices in a mesh: parts: 2 (over x), seq: 8 (over z, y), dp: 2 (over core).
Axes of the slice: x: 2, y: 2, z: 4, core: 2. Of those that a mesh axis runs over, the one named last changes fastest.
Arguments:
- queries: bfloat16 [4, 2048, 1024], P(('parts', 'dp'), 'seq'), parts along dimension 0, may hold values from -8 to 8
- key_states: bfloat16 [4, 2048, 1024], P(('parts', 'dp'), 'seq'), parts along dimension 0, may hold values from -8 to 8
- value_states: bfloat16 [4, 2048, 1024], P(('parts', 'dp'), 'seq'), parts along dimension 0, may hold values from -6 to 6
- out_grad: bfloat16 [4, 2048, 1024], P(('parts', 'dp'), 'seq'), parts along dimension 0, may hold values from -1.5 to 1.5
- layer_input: bfloat16 [4, 2048, 2048], P(('parts', 'dp'), 'seq'), parts along dimension 0, may hold values from -6 to 6
Outputs:
- weight_grad: float32 [4096, 1024], P(('parts', 'seq', 'dp')), parts along dimension 0
The draws below stay inside these ranges and needn't reach their ends.
There are 2 independent parts, one for each index of `parts`. The reference program is written for one: setup_inputs(seed, part) draws one part's arguments, and reference() takes and returns one part's arrays. A program takes and returns all parts, laid end to end along the dimension named above; each array names one. Nothing has to cross between parts.
All inputs are finite; a program needn't handle non-finite values.
Results may differ from the reference program's by a relative error of at most 0.0041.
Values may be sent and summed in bfloat16 or wider, within the bound.
No kernel may reach another device: no remote copies, remote signals or barrier semaphores. Data moves between devices by JAX's collectives and lax.ppermute only.
A program may use at most 192 MiB of HBM per device.

```python
import math
import jax
import jax.numpy as jnp
from jax import lax

D = 2048
HEADS = 8
HEAD_DIM = 128
HALF = 1024
TOK_DEV = 256
HD = 1024
TOKENS = 2048
DOCS = 2
N_SEQ = 8


def draw_queries(key, part):
    normal_part = jax.random.normal(jax.random.fold_in(key, 1), (DOCS, TOKENS, HD), jnp.float32)
    spread = jnp.exp(jax.random.uniform(jax.random.fold_in(key, 2), (DOCS, TOKENS, 1), jnp.float32, math.log(0.4), math.log(2.0)))
    values = normal_part * spread
    return jnp.clip(values, -8.0, 8.0).astype(jnp.bfloat16)


def draw_key_states(key, part):
    normal_part = jax.random.normal(jax.random.fold_in(key, 5), (DOCS, TOKENS, HD), jnp.float32)
    spread = jnp.exp(jax.random.uniform(jax.random.fold_in(key, 6), (DOCS, TOKENS, 1), jnp.float32, math.log(0.4), math.log(2.0)))
    values = normal_part * spread
    return jnp.clip(values, -8.0, 8.0).astype(jnp.bfloat16)


def raised(values, stream_key, source, target, blocks, factor):
    def block_of(dim):
        return (jnp.arange(values.shape[dim]) // (values.shape[dim] // blocks)).reshape((-1,) + (1,) * (values.ndim - 1 - dim))

    near = jax.random.permutation(stream_key, blocks)[block_of(target)]
    second = (block_of(target) + blocks // 2) % blocks
    return jnp.where((block_of(source) == near) | (block_of(source) == second), factor * values, values)


def steps_of(key, shape, cuts, smallest, top_value):
    factor_of = 1.0
    for axis_at, blocks in cuts:
        draws = jax.random.uniform(jax.random.fold_in(jax.random.fold_in(key, 6), axis_at), (blocks,), jnp.float32, smallest / len(cuts), top_value / len(cuts))
        factor_of = factor_of * jnp.repeat(jnp.exp(draws), shape[axis_at] // blocks).reshape((-1,) + (1,) * (len(shape) - 1 - axis_at))
    return factor_of


def bell_draw(own_key, dims, scale, most, split=(), held_as=jnp.bfloat16):
    result = scale * jax.random.normal(own_key, dims, jnp.float32)
    if split:
        result = result * steps_of(own_key, dims, split, -0.22, 0.18)
    return jnp.clip(result, -most, most).astype(held_as)


def bell_draw_with(rng, extent, scale, most, cuts, heavy, dtype=jnp.bfloat16):
    values = scale * jax.random.normal(rng, extent, jnp.float32)
    if cuts:
        values = values * steps_of(rng, extent, cuts, -0.22, 0.18)
    return jnp.clip(raised(values, jax.random.fold_in(rng, 3), *heavy), -most, most).astype(dtype)


def setup_inputs(seed: int = 0, part: int = 0) -> dict:
    key_of = jax.random.split(jax.random.key(seed), 6)
    part_splits = jax.random.split(jax.random.fold_in(key_of[5], part), 6)
    return {
        "queries": draw_queries(jax.random.fold_in(jax.random.fold_in(key_of[5], part), 71), part),
        "key_states": draw_key_states(jax.random.fold_in(jax.random.fold_in(key_of[5], part), 71), part),
        "value_states": bell_draw(part_splits[2], (DOCS, TOKENS, HD), 1.0, 6.0, ((0, 2), (1, 8))),
        "out_grad": bell_draw(part_splits[3], (DOCS, TOKENS, HD), 0.25, 1.5, ((0, 2), (1, 8))),
        "layer_input": bell_draw_with(part_splits[4], (DOCS, TOKENS, D), 1.0, 6.0, ((0, 2), (1, 8)), (1, 2, 8, 2.0)),
    }


def shard_term(query_doc, key_pad, value_pad, grad_doc, input_pad, shard):
    begin_row = (shard * TOK_DEV).astype(jnp.int32)
    window = TOK_DEV + 2 * HALF
    inverse_root = 1.0 / math.sqrt(HEAD_DIM)
    query_rows = lax.dynamic_slice_in_dim(query_doc, begin_row, TOK_DEV, 0).astype(jnp.float32).reshape(TOK_DEV, HEADS, HEAD_DIM)
    grad_rows = lax.dynamic_slice_in_dim(grad_doc, begin_row, TOK_DEV, 0).astype(jnp.float32).reshape(TOK_DEV, HEADS, HEAD_DIM)
    key_rows = lax.dynamic_slice_in_dim(key_pad, begin_row, window, 0).astype(jnp.float32).reshape(window, HEADS, HEAD_DIM)
    value_rows = lax.dynamic_slice_in_dim(value_pad, begin_row, window, 0).astype(jnp.float32).reshape(window, HEADS, HEAD_DIM)
    input_rows = lax.dynamic_slice_in_dim(input_pad, begin_row, window, 0)
    offsets = jnp.arange(window)[None, :] - jnp.arange(TOK_DEV)[:, None]
    position = begin_row - HALF + jnp.arange(window)
    visible = (offsets >= 0) & (offsets <= 2 * HALF) & (position >= 0)[None, :] & (position < TOKENS)[None, :]
    scores = jnp.einsum('ihe,jhe->hij', query_rows, key_rows) * inverse_root
    scores = jnp.where(visible[None], scores, -1e+30)
    row_max = lax.optimization_barrier(jnp.max(scores, axis=2, keepdims=True))
    weights = jnp.where(visible[None], jnp.exp(scores - row_max), 0.0)
    probs = weights / lax.optimization_barrier(jnp.sum(weights, axis=2, keepdims=True))
    dprobs = jnp.einsum('ihe,jhe->hij', grad_rows, value_rows)
    row_delta = lax.optimization_barrier(jnp.sum(probs * dprobs, axis=2, keepdims=True))
    dscores = probs * (dprobs - row_delta)
    dscores_low = lax.optimization_barrier(dscores.astype(jnp.bfloat16)).astype(jnp.float32)
    key_grad = jnp.einsum('hij,ihe->jhe', dscores_low, query_rows) * inverse_root
    partial_value = key_grad.reshape(window, HD).astype(jnp.bfloat16)
    return jnp.dot(input_rows.T, partial_value, preferred_element_type=jnp.float32)

def reference(queries, key_states, value_states, out_grad, layer_input):
    accumulated = jnp.zeros((D, HD), jnp.float32)
    padding = ((HALF, HALF), (0, 0))
    for document in range(DOCS):
        key_pad = jnp.pad(key_states[document], padding)
        value_pad = jnp.pad(value_states[document], padding)
        input_pad = jnp.pad(layer_input[document], padding)
        query_doc = queries[document]
        grad_doc = out_grad[document]

        def add_shard(shard, carried):
            return carried + shard_term(query_doc, key_pad, value_pad, grad_doc, input_pad, shard)
        accumulated = lax.fori_loop(0, N_SEQ, add_shard, accumulated)
    return accumulated
```

```python
import functools
import math

import jax
import jax.numpy as jnp
from jax import lax
from jax.experimental import pallas as pl
from jax.experimental.pallas import tpu as pltpu
from jax.sharding import PartitionSpec as P

HEADS = 8
HEAD_DIM = 128
HALF = 1024
NEG = -1e30
NT = (((1,), (1,)), ((), ()))


def exchange(value, axis, distance):
    count = lax.axis_size(axis)
    return lax.ppermute(value, axis, [(source, source ^ distance) for source in range(count)])


def fold_rows(value, op):
    rows = value.shape[0]
    total = value[0:8]
    for start in range(8, rows, 8):
        total = op(total, value[start : start + 8])
    return total


def head_kernel(tok, halo, groups, place, *refs):
    pieces = refs[0:HEADS]
    refs = refs[HEADS:]
    if halo:
        halves, refs = refs[0:2], refs[2:]
        out_refs, refs = refs[0:1], refs[1:]
    else:
        out_refs, refs = refs[0 : HEADS // 2], refs[HEADS // 2 :]
    query_ref, key_ref, value_ref, grad_ref, score_ref, dprob_ref, total_ref, sem = refs
    me = place[0]
    group_rows = HEADS * tok
    blocks = (group_rows + 2 * halo) // tok
    reach = HALF // tok
    inverse_root = 1.0 / math.sqrt(HEAD_DIM)
    scale = inverse_root * math.log2(math.e)

    copies = []
    for distance in range(HEADS):
        start = pl.multiple_of((me ^ distance) * tok, tok)
        targets = (
            query_ref.at[pl.ds(start, tok)],
            key_ref.at[pl.ds(start + halo, tok)],
            value_ref.at[pl.ds(start + halo, tok)],
            grad_ref.at[pl.ds(start, tok)],
        )
        for index, target in enumerate(targets):
            copies.append(pltpu.make_async_copy(pieces[distance].at[index], target, sem))
    if halo:
        for side, start in ((0, 0), (1, halo + group_rows)):
            for index, target in enumerate((key_ref, value_ref)):
                copies.append(
                    pltpu.make_async_copy(
                        halves[side].at[index], target.at[pl.ds(start, halo)], sem
                    )
                )
    for copy in copies:
        copy.start()
    total_ref[...] = jnp.zeros_like(total_ref)
    for copy in copies:
        copy.wait()

    row = lax.broadcasted_iota(jnp.int32, (tok, tok), 0)
    col = lax.broadcasted_iota(jnp.int32, (tok, tok), 1)
    for b in range(HEADS):
        slot = b % 2
        query = query_ref[b * tok : (b + 1) * tok]
        grad = grad_ref[b * tok : (b + 1) * tok]
        shift = halo // tok
        window = range(max(0, b + shift - reach), min(blocks, b + shift + reach + 1))
        top = None
        for at, kb in enumerate(window):
            key = key_ref[kb * tok : (kb + 1) * tok]
            score = lax.dot_general(key, query, NT, preferred_element_type=jnp.float32)
            if kb - shift == b - reach:
                score = jnp.where(row >= col, score, NEG)
            if kb - shift == b + reach:
                score = jnp.where(row <= col, score, NEG)
            if kb < shift:
                score = jnp.where(place[1] > 0, score, NEG)
            if kb - shift >= HEADS:
                score = jnp.where(place[1] < groups - 1, score, NEG)
            score_ref[slot, at * tok : (at + 1) * tok] = score
            part = fold_rows(score, jnp.maximum)
            top = part if top is None else jnp.maximum(top, part)
        top = jnp.max(top, axis=0, keepdims=True) * scale
        weight_sum = jnp.zeros((8, tok), jnp.float32)
        delta_sum = jnp.zeros((8, tok), jnp.float32)
        for at, kb in enumerate(window):
            value = value_ref[kb * tok : (kb + 1) * tok]
            dprob = lax.dot_general(value, grad, NT, preferred_element_type=jnp.float32)
            weight = jnp.exp2(score_ref[slot, at * tok : (at + 1) * tok] * scale - top)
            score_ref[slot, at * tok : (at + 1) * tok] = weight
            dprob_ref[slot, at * tok : (at + 1) * tok] = dprob
            weight_sum = weight_sum + fold_rows(weight, jnp.add)
            delta_sum = delta_sum + fold_rows(weight * dprob, jnp.add)
        inverse = 1.0 / jnp.sum(weight_sum, axis=0, keepdims=True)
        delta = jnp.sum(delta_sum, axis=0, keepdims=True) * inverse
        for at, kb in enumerate(window):
            prob = score_ref[slot, at * tok : (at + 1) * tok] * inverse
            dscore = prob * (dprob_ref[slot, at * tok : (at + 1) * tok] - delta)
            total_ref[kb * tok : (kb + 1) * tok] += jnp.dot(
                dscore.astype(jnp.bfloat16), query, preferred_element_type=jnp.float32
            )
    if halo:
        out_refs[0][...] = total_ref[...] * inverse_root
    else:
        pair = 2 * tok
        for distance in range(HEADS // 2):
            start = pl.multiple_of(((me // 2) ^ distance) * pair, pair)
            out_refs[distance][...] = (
                total_ref[pl.ds(start, pair)] * inverse_root
            ).astype(jnp.bfloat16)


def head_grads(place, pieces, halves, groups):
    tok = pieces[0].shape[1]
    halo = HALF if halves else 0
    rows = HEADS * tok
    span = rows + 2 * halo
    window = min(span, tok + 2 * HALF)
    if halo:
        out_shape = [jax.ShapeDtypeStruct((span, HEAD_DIM), jnp.float32)]
    else:
        out_shape = [jax.ShapeDtypeStruct((2 * tok, HEAD_DIM), jnp.bfloat16)] * (HEADS // 2)
    any_spec = pl.BlockSpec(memory_space=pl.ANY)
    return pl.pallas_call(
        functools.partial(head_kernel, tok, halo, groups),
        out_shape=out_shape,
        in_specs=[pl.BlockSpec(memory_space=pltpu.SMEM)]
        + [any_spec] * (len(pieces) + len(halves)),
        out_specs=[pl.BlockSpec(memory_space=pltpu.VMEM)] * len(out_shape),
        scratch_shapes=[
            pltpu.VMEM((rows, HEAD_DIM), jnp.bfloat16),
            pltpu.VMEM((span, HEAD_DIM), jnp.bfloat16),
            pltpu.VMEM((span, HEAD_DIM), jnp.bfloat16),
            pltpu.VMEM((rows, HEAD_DIM), jnp.bfloat16),
            pltpu.VMEM((2, window, tok), jnp.float32),
            pltpu.VMEM((2, window, tok), jnp.float32),
            pltpu.VMEM((span, HEAD_DIM), jnp.float32),
            pltpu.SemaphoreType.DMA,
        ],
        compiler_params=pltpu.CompilerParams(vmem_limit_bytes=40 * 2**20),
        cost_estimate=pl.CostEstimate(
            flops=6 * rows * window * HEAD_DIM,
            bytes_accessed=8 * rows * HEAD_DIM,
            transcendentals=rows * window,
        ),
        name="head_grads",
    )(place, *pieces, *halves)


def weight_kernel(place, input_ref, *refs):
    count = HEADS // 2
    own, other = refs[0:count], refs[count : 2 * count]
    out_ref, near_ref, grad_ref = refs[2 * count :]
    column = place[0] // 2
    core = place[2]
    tokens = own[0].shape[0]
    for distance in range(count):
        start = pl.multiple_of((column ^ distance) * HEAD_DIM, HEAD_DIM)
        at = pl.multiple_of(core * tokens, tokens)
        grad_ref[pl.ds(at, tokens), pl.ds(start, HEAD_DIM)] = own[distance][...]
        at = pl.multiple_of((1 - core) * tokens, tokens)
        grad_ref[pl.ds(at, tokens), pl.ds(start, HEAD_DIM)] = other[distance][...]
    for target in range(input_ref.shape[0]):
        product = jnp.dot(
            input_ref[target], grad_ref[...], preferred_element_type=jnp.float32
        )
        out_ref[target] = product.astype(out_ref.dtype)
        if target == 0:
            near_ref[...] = product


def weight_parts(place, inputs, own, other, dtype):
    targets, share, depth = inputs.shape
    width = len(own) * HEAD_DIM
    vmem = pl.BlockSpec(memory_space=pltpu.VMEM)
    return pl.pallas_call(
        weight_kernel,
        out_shape=[
            jax.ShapeDtypeStruct((targets, share, width), dtype),
            jax.ShapeDtypeStruct((share, width), jnp.float32),
        ],
        in_specs=[pl.BlockSpec(memory_space=pltpu.SMEM)] + [vmem] * (1 + len(own) + len(other)),
        out_specs=[vmem, vmem],
        scratch_shapes=[pltpu.VMEM((depth, width), jnp.bfloat16)],
        compiler_params=pltpu.CompilerParams(vmem_limit_bytes=24 * 2**20),
        cost_estimate=pl.CostEstimate(
            flops=2 * targets * share * depth * width,
            bytes_accessed=2 * depth * (width + targets * share),
            transcendentals=0,
        ),
        name="weight_parts",
    )(place, inputs, *own, *other)


def ordered(first, own, other, axis):
    return jnp.where(first == 0, jnp.stack([own, other], axis), jnp.stack([other, own], axis))


def gathered_inputs(layer_input, me, parity, core, groups):
    tok, width = layer_input.shape
    columns = lax.axis_size("seq") // 2
    share = width // (columns * 4)
    shaped = layer_input.reshape(tok, columns, 2, 2, share)
    keep = lax.dynamic_index_in_dim(shaped, parity, 2, keepdims=False)
    give = lax.dynamic_index_in_dim(shaped, 1 - parity, 2, keepdims=False)
    both = ordered(parity, keep, exchange(give, "seq", 1), 0)
    both = both.reshape(2 * tok, columns, 2, share)
    keep = lax.dynamic_index_in_dim(both, core, 2, keepdims=False)
    give = lax.dynamic_index_in_dim(both, 1 - core, 2, keepdims=False)
    full = ordered(core, keep, exchange(give, "dp", 1), 0)
    full = full.reshape(4 * tok, columns, share).transpose(1, 2, 0)
    if groups == 1:
        here = me // 2
        full = jnp.stack(
            [
                lax.dynamic_index_in_dim(full, here ^ distance, 0, keepdims=False)
                for distance in range(columns)
            ]
        )
    return full


def local(queries, key_states, value_states, out_grad, layer_input):
    seq_count = lax.axis_size("seq")
    groups = seq_count // HEADS
    tok = queries.shape[1]
    index = lax.axis_index("seq")
    core = lax.axis_index("dp")
    me = index % HEADS
    group = index // HEADS
    parity = index % 2
    place = jnp.stack([me, group, core]).astype(jnp.int32)

    def piece(distance):
        start = (me ^ distance) * HEAD_DIM
        return jnp.stack(
            [
                lax.dynamic_slice_in_dim(array[0], start, HEAD_DIM, 1)
                for array in (queries, key_states, value_states, out_grad)
            ]
        )

    pieces = [None] * HEADS
    for distance in (6, 7, 4, 5, 2, 3, 1):
        pieces[distance] = exchange(piece(distance), "seq", distance)
    pieces[0] = piece(0)
    inputs = gathered_inputs(layer_input[0], me, parity, core, groups)

    if groups == 1:
        grads = head_grads(place, pieces, [], groups)
    else:
        ordered_pieces = jnp.stack(pieces)
        rows = jnp.stack(
            [
                lax.dynamic_index_in_dim(ordered_pieces, me ^ block, 0, keepdims=False)
                for block in range(HEADS)
            ]
        )
        rows = rows[:, 1:3].transpose(1, 0, 2, 3).reshape(2, HEADS * tok, HEAD_DIM)
        ahead = [(source, source + HEADS) for source in range(seq_count - HEADS)]
        back = [(source + HEADS, source) for source in range(seq_count - HEADS)]
        before = lax.ppermute(rows[:, -HALF:], "seq", ahead)
        after = lax.ppermute(rows[:, :HALF], "seq", back)
        span = head_grads(place, pieces, [before, after], groups)[0]
        from_after = lax.ppermute(span[:HALF].astype(jnp.bfloat16), "seq", back)
        from_before = lax.ppermute(span[-HALF:].astype(jnp.bfloat16), "seq", ahead)
        inner = span[HALF:-HALF]
        inner = inner.at[-HALF:].add(from_after.astype(jnp.float32))
        inner = inner.at[:HALF].add(from_before.astype(jnp.float32))
        inner = inner.astype(jnp.bfloat16)
        grads = [
            lax.dynamic_slice_in_dim(inner, ((me // 2) ^ distance) * 2 * tok, 2 * tok, 0)
            for distance in range(HEADS // 2)
        ]

    near = [grads[0]] + [None] * (HEADS // 2 - 1)
    for distance in (3, 2, 1):
        near[distance] = exchange(grads[distance], "seq", 2 * distance)

    def reduced(own):
        stacked = jnp.stack(own)
        swapped = exchange(stacked, "dp", 1)
        other = [swapped[distance] for distance in range(HEADS // 2)]
        if groups > 1:
            full = weight_parts(place, inputs, own, other, jnp.float32)[0]
            full = full.reshape(-1, full.shape[2])
            members = [list(range(first, seq_count, 2)) for first in (0, 1)]
            return lax.psum_scatter(
                full, "seq", scatter_dimension=0, axis_index_groups=members, tiled=True
            )
        parts, total = weight_parts(place, inputs, own, other, jnp.bfloat16)
        for distance in (3, 2, 1):
            total = total + exchange(parts[distance], "seq", 2 * distance).astype(jnp.float32)
        return total

    stacked = jnp.stack(near)
    far = exchange(stacked, "seq", 1)
    first = reduced(near)
    second = reduced([far[distance] for distance in range(HEADS // 2)])
    share, width = first.shape
    shape = (share, HEADS // 2, HEAD_DIM)
    result = ordered(parity, first.reshape(shape), second.reshape(shape), 2)
    return result.reshape(share, 2 * width)


def solution(mesh):
    spec = P(("parts", "dp"), "seq", None)
    out_specs = P(("parts", "seq", "dp"), None)
    return jax.shard_map(
        local, mesh=mesh, in_specs=(spec,) * 5, out_specs=out_specs, check_vma=False
    )
```

```python
import functools
import math

import jax
import jax.numpy as jnp
from jax import lax
from jax.experimental import pallas as pl
from jax.experimental.pallas import tpu as pltpu
from jax.sharding import PartitionSpec as P

HEADS = 8
HEAD_DIM = 128
HALF = 1024
NEG = -1e30
CHUNK = 4
NT = (((1,), (1,)), ((), ()))


def exchange(value, axis, distance):
    count = lax.axis_size(axis)
    return lax.ppermute(value, axis, [(source, source ^ distance) for source in range(count)])


def fold_rows(value, op):
    rows = value.shape[0]
    total = value[0:8]
    for start in range(8, rows, 8):
        total = op(total, value[start : start + 8])
    return total


def split_kernel(place, left, right, *refs):
    outs, sem = refs[:-1], refs[-1]
    copies = []
    for distance, out in enumerate(outs, 1):
        start = pl.multiple_of((place[0] ^ distance) * HEAD_DIM, HEAD_DIM)
        for index, array in enumerate((left, right)):
            copies.append(
                pltpu.make_async_copy(array.at[:, pl.ds(start, HEAD_DIM)], out.at[index], sem)
            )
    for copy in copies:
        copy.start()
    for copy in copies:
        copy.wait()


def split_heads(place, left, right):
    any_spec = pl.BlockSpec(memory_space=pl.ANY)
    tok = left.shape[0]
    shape = jax.ShapeDtypeStruct((2, tok, HEAD_DIM), left.dtype)
    return pl.pallas_call(
        split_kernel,
        out_shape=[shape] * (HEADS - 1),
        in_specs=[pl.BlockSpec(memory_space=pltpu.SMEM), any_spec, any_spec],
        out_specs=[any_spec] * (HEADS - 1),
        scratch_shapes=[pltpu.SemaphoreType.DMA],
        cost_estimate=pl.CostEstimate(
            flops=0, bytes_accessed=4 * left.size * left.dtype.itemsize, transcendentals=0
        ),
        name="split_heads",
    )(place, left, right)


def head_block(dims, place, b, query, grad, key_ref, value_ref, score_ref, dprob_ref, total_ref):
    tok, halo, groups = dims
    shift = halo // tok
    reach = HALF // tok
    scale = math.log2(math.e) / math.sqrt(HEAD_DIM)
    row = lax.broadcasted_iota(jnp.int32, (tok, tok), 0)
    col = lax.broadcasted_iota(jnp.int32, (tok, tok), 1)
    if halo:
        first, count, lowest = b + shift - reach, 2 * reach + 1, 0
    else:
        first = max(0, b - reach)
        count = min(HEADS, b + reach + 1) - first
        lowest = b - reach - first
    chunks = [range(start, min(start + CHUNK, count)) for start in range(0, count, CHUNK)]

    def rows_of(chunk):
        start = (first + chunk[0]) * tok
        return pl.ds(pl.multiple_of(start, tok) if halo else start, len(chunk) * tok)

    def held(at):
        return slice(at * tok, (at + 1) * tok)

    top = None
    for chunk in chunks:
        scores = lax.dot_general(
            key_ref[rows_of(chunk)], query, NT, preferred_element_type=jnp.float32
        )
        for at in chunk:
            score = scores[held(at - chunk[0])]
            if at == lowest:
                score = jnp.where(row >= col, score, NEG)
            if at == lowest + 2 * reach:
                score = jnp.where(row <= col, score, NEG)
            if halo:
                inside = (first + at >= shift) | (place[1] > 0)
                inside &= (first + at < shift + HEADS) | (place[1] < groups - 1)
                score = jnp.where(inside, score, NEG)
            score_ref[held(at)] = score
            part = fold_rows(score, jnp.maximum)
            top = part if top is None else jnp.maximum(top, part)
    top = jnp.max(top, axis=0, keepdims=True) * scale
    weight_sum = jnp.zeros((8, tok), jnp.float32)
    delta_sum = jnp.zeros((8, tok), jnp.float32)
    for chunk in chunks:
        dprobs = lax.dot_general(
            value_ref[rows_of(chunk)], grad, NT, preferred_element_type=jnp.float32
        )
        for at in chunk:
            dprob = dprobs[held(at - chunk[0])]
            weight = jnp.exp2(score_ref[held(at)] * scale - top)
            score_ref[held(at)] = weight
            dprob_ref[held(at)] = dprob
            weight_sum = weight_sum + fold_rows(weight, jnp.add)
            delta_sum = delta_sum + fold_rows(weight * dprob, jnp.add)
    inverse = 1.0 / jnp.sum(weight_sum, axis=0, keepdims=True)
    delta = jnp.sum(delta_sum, axis=0, keepdims=True) * inverse
    for chunk in chunks:
        held_rows = slice(chunk[0] * tok, (chunk[-1] + 1) * tok)
        prob = score_ref[held_rows] * inverse
        dscore = prob * (dprob_ref[held_rows] - delta)
        total_ref[rows_of(chunk)] += jnp.dot(
            dscore.astype(jnp.bfloat16), query, preferred_element_type=jnp.float32
        )


def query_blocks(dims, place, distances, sources, refs):
    tok = dims[0]
    me = place[0]
    key_ref, value_ref, query_ref, grad_ref, score_ref, dprob_ref, total_ref, sem = refs
    copies = []
    for slot, source in enumerate(sources):
        rows = slice(slot * tok, (slot + 1) * tok)
        for target, piece in zip((query_ref, grad_ref), source):
            copies.append(pltpu.make_async_copy(piece, target.at[rows], sem))
    for copy in copies:
        copy.start()
    yield
    for copy in copies:
        copy.wait()

    def block(at, b, half):
        slot = 2 * at + ((me % 2) ^ half)
        rows = pl.ds(pl.multiple_of(slot * tok, tok), tok)
        head_block(
            dims, place, b, query_ref[rows], grad_ref[rows], key_ref, value_ref,
            score_ref.at[half], dprob_ref.at[half], total_ref,
        )

    for at, distance in enumerate(distances):
        pair = (me // 2) ^ distance
        if dims[1]:

            @pl.loop(0, 2)
            def _(half, at=at, pair=pair):
                block(at, 2 * pair + half, half)

            continue
        for index in range(HEADS // 2):

            @pl.when(pair == index)
            def _(at=at, index=index):
                for half in range(2):
                    block(at, 2 * index + half, half)

    yield


def first_kernel(dims, distances, place, *refs):
    tok, halo, _ = dims
    me = place[0]
    query, key, value, grad = refs[:4]
    key_values, refs = refs[4 : 3 + HEADS], refs[3 + HEADS :]
    count = 2 * len(distances) - 1
    others, refs = refs[:count], refs[count:]
    if halo:
        halves, refs = refs[:2], refs[2:]
    total_ref, key_ref, value_ref, query_ref, grad_ref, score_ref, dprob_ref, sem = refs
    mine = pl.ds(pl.multiple_of(me * HEAD_DIM, HEAD_DIM), HEAD_DIM)
    copies = []
    for distance in range(HEADS):
        rows = pl.ds(pl.multiple_of((me ^ distance) * tok + halo, tok), tok)
        pair = (key, value)
        if distance:
            pair = [key_values[distance - 1].at[index] for index in range(2)]
        else:
            pair = (key.at[:, mine], value.at[:, mine])
        for source, target in zip(pair, (key_ref, value_ref)):
            copies.append(pltpu.make_async_copy(source, target.at[rows], sem))
    if halo:
        for side, start in ((0, 0), (1, halo + HEADS * tok)):
            for index, target in enumerate((key_ref, value_ref)):
                copies.append(
                    pltpu.make_async_copy(
                        halves[side].at[index], target.at[pl.ds(start, halo)], sem
                    )
                )
    for copy in copies:
        copy.start()
    sources = [(query.at[:, mine], grad.at[:, mine])]
    sources += [(other.at[0], other.at[1]) for other in others]
    steps = query_blocks(
        dims, place, distances, sources,
        (key_ref, value_ref, query_ref, grad_ref, score_ref, dprob_ref, total_ref, sem),
    )
    next(steps)
    total_ref[...] = jnp.zeros_like(total_ref)
    for copy in copies:
        copy.wait()
    next(steps)


def later_kernel(dims, distances, last, place, before_ref, key_ref, value_ref, *refs):
    tok, halo, _ = dims
    count = 2 * len(distances)
    others, refs = refs[:count], refs[count:]
    split = last and not halo
    if split:
        outs, refs = refs[: HEADS // 2], refs[HEADS // 2 :]
        total_ref, refs = refs[0], refs[1:]
    else:
        total_ref, refs = refs[0], refs[1:]
    sources = [(other.at[0], other.at[1]) for other in others]
    query_ref, grad_ref, score_ref, dprob_ref, sem = refs
    steps = query_blocks(
        dims, place, distances, sources,
        (key_ref, value_ref, query_ref, grad_ref, score_ref, dprob_ref, total_ref, sem),
    )
    next(steps)
    total_ref[...] = before_ref[...]
    next(steps)
    inverse_root = 1.0 / math.sqrt(HEAD_DIM)
    if split:
        pair = 2 * tok
        for distance, out in enumerate(outs):
            start = pl.multiple_of(((place[0] // 2) ^ distance) * pair, pair)
            out[...] = (total_ref[pl.ds(start, pair)] * inverse_root).astype(jnp.bfloat16)
    elif last:
        total_ref[...] = total_ref[...] * inverse_root


def head_grads(place, arrays, key_values, query_grads, halves, groups):
    tok = arrays[0].shape[0]
    halo = HALF if halves else 0
    dims = (tok, halo, groups)
    span = HEADS * tok + 2 * halo
    window = min(span, tok + 2 * HALF)
    any_spec = pl.BlockSpec(memory_space=pl.ANY)
    vmem = pl.BlockSpec(memory_space=pltpu.VMEM)
    smem = pl.BlockSpec(memory_space=pltpu.SMEM)
    total = jax.ShapeDtypeStruct((span, HEAD_DIM), jnp.float32)
    low = jax.ShapeDtypeStruct((span, HEAD_DIM), jnp.bfloat16)
    piece = jax.ShapeDtypeStruct((2 * tok, HEAD_DIM), jnp.bfloat16)
    params = pltpu.CompilerParams(vmem_limit_bytes=24 * 2**20)

    def scratch(pairs):
        return [
            pltpu.VMEM((2 * pairs * tok, HEAD_DIM), jnp.bfloat16),
            pltpu.VMEM((2 * pairs * tok, HEAD_DIM), jnp.bfloat16),
            pltpu.VMEM((2, window, tok), jnp.float32),
            pltpu.VMEM((2, window, tok), jnp.float32),
        ]

    def cost(pairs):
        return pl.CostEstimate(
            flops=12 * pairs * tok * window * HEAD_DIM,
            bytes_accessed=8 * span * HEAD_DIM,
            transcendentals=2 * pairs * tok * window,
        )

    sem = [pltpu.SemaphoreType.DMA]
    state = pl.pallas_call(
        functools.partial(first_kernel, dims, (0, 1)),
        out_shape=[total, low, low],
        in_specs=[smem] + [any_spec] * (4 + HEADS - 1 + 3 + len(halves)),
        out_specs=[vmem] * 3,
        scratch_shapes=scratch(2) + sem,
        compiler_params=params,
        cost_estimate=cost(2),
        name="head_first",
    )(place, *arrays, *key_values, *query_grads[:3], *halves)
    for distance in (2, 3):
        last = distance == 3
        split = last and not halo
        others = query_grads[2 * distance - 1 : 2 * distance + 1]
        out = pl.pallas_call(
            functools.partial(later_kernel, dims, (distance,), last),
            out_shape=[piece] * (HEADS // 2) if split else [total],
            in_specs=[smem] + [vmem] * 3 + [any_spec] * 2,
            out_specs=[vmem] * (HEADS // 2 if split else 1),
            scratch_shapes=([pltpu.VMEM(total.shape, total.dtype)] if split else [])
            + scratch(1)
            + sem,
            compiler_params=params,
            cost_estimate=cost(1),
            name="head_later",
        )(place, *state, *others)
        state = [out[0], *state[1:]]
    return out if split else out[0]


def weight_kernel(place, input_ref, *refs):
    count = HEADS // 2
    own, other = refs[0:count], refs[count : 2 * count]
    near_ref, grad_ref = refs[-2:]
    out_refs = refs[2 * count : -2]
    column = place[0] // 2
    core = place[2]
    tokens = own[0].shape[0]
    for distance in range(count):
        start = pl.multiple_of((column ^ distance) * HEAD_DIM, HEAD_DIM)
        at = pl.multiple_of(core * tokens, tokens)
        grad_ref[pl.ds(at, tokens), pl.ds(start, HEAD_DIM)] = own[distance][...]
        at = pl.multiple_of((1 - core) * tokens, tokens)
        grad_ref[pl.ds(at, tokens), pl.ds(start, HEAD_DIM)] = other[distance][...]
    for target in range(input_ref.shape[0]):
        product = jnp.dot(
            input_ref[target], grad_ref[...], preferred_element_type=jnp.float32
        )
        out_refs[target][...] = product.astype(out_refs[target].dtype)
        if target == 0:
            near_ref[...] = product


def weight_parts(place, inputs, own, other, dtype):
    targets, share, depth = inputs.shape
    width = len(own) * HEAD_DIM
    vmem = pl.BlockSpec(memory_space=pltpu.VMEM)
    return pl.pallas_call(
        weight_kernel,
        out_shape=[jax.ShapeDtypeStruct((share, width), dtype)] * targets
        + [jax.ShapeDtypeStruct((share, width), jnp.float32)],
        in_specs=[pl.BlockSpec(memory_space=pltpu.SMEM)] + [vmem] * (1 + len(own) + len(other)),
        out_specs=[vmem] * (targets + 1),
        scratch_shapes=[pltpu.VMEM((depth, width), jnp.bfloat16)],
        compiler_params=pltpu.CompilerParams(vmem_limit_bytes=24 * 2**20),
        cost_estimate=pl.CostEstimate(
            flops=2 * targets * share * depth * width,
            bytes_accessed=2 * depth * (width + targets * share),
            transcendentals=0,
        ),
        name="weight_parts",
    )(place, inputs, *own, *other)


def sum_kernel(place, *refs):
    out_ref = refs[-1]
    count = HEADS // 2
    for side in range(2):
        total = refs[side * count][...]
        for index in range(1, count):
            total = total + refs[side * count + index][...].astype(jnp.float32)
        parity = (place[0] % 2) ^ side
        for column in range(count):
            start = pl.multiple_of((2 * column + parity) * HEAD_DIM, HEAD_DIM)
            out_ref[:, pl.ds(start, HEAD_DIM)] = total[
                :, column * HEAD_DIM : (column + 1) * HEAD_DIM
            ]


def summed(place, near, far):
    share, width = near[0].shape
    vmem = pl.BlockSpec(memory_space=pltpu.VMEM)
    return pl.pallas_call(
        sum_kernel,
        out_shape=jax.ShapeDtypeStruct((share, 2 * width), jnp.float32),
        in_specs=[pl.BlockSpec(memory_space=pltpu.SMEM)] + [vmem] * (len(near) + len(far)),
        out_specs=vmem,
        name="summed",
    )(place, *near, *far)


def ordered(first, own, other, axis):
    return jnp.where(first == 0, jnp.stack([own, other], axis), jnp.stack([other, own], axis))


def gathered_inputs(layer_input, me, parity, core, groups):
    tok, width = layer_input.shape
    columns = lax.axis_size("seq") // 2
    share = width // (columns * 4)
    shaped = layer_input.reshape(tok, columns, 2, 2, share)
    keep = lax.dynamic_index_in_dim(shaped, parity, 2, keepdims=False)
    give = lax.dynamic_index_in_dim(shaped, 1 - parity, 2, keepdims=False)
    both = ordered(parity, keep, exchange(give, "seq", 1), 0)
    both = both.reshape(2 * tok, columns, 2, share)
    keep = lax.dynamic_index_in_dim(both, core, 2, keepdims=False)
    give = lax.dynamic_index_in_dim(both, 1 - core, 2, keepdims=False)
    full = ordered(core, keep, exchange(give, "dp", 1), 0)
    full = full.reshape(4 * tok, columns, share).transpose(1, 2, 0)
    if groups == 1:
        here = me // 2
        full = jnp.stack(
            [
                lax.dynamic_index_in_dim(full, here ^ distance, 0, keepdims=False)
                for distance in range(columns)
            ]
        )
    return full


def local(queries, key_states, value_states, out_grad, layer_input):
    seq_count = lax.axis_size("seq")
    groups = seq_count // HEADS
    tok = queries.shape[1]
    index = lax.axis_index("seq")
    core = lax.axis_index("dp")
    me = index % HEADS
    group = index // HEADS
    parity = index % 2
    place = jnp.stack([me, group, core]).astype(jnp.int32)
    arrays = [array[0] for array in (queries, key_states, value_states, out_grad)]

    def sent(pieces):
        received = [None] * HEADS
        for distance in (6, 7, 4, 5, 2, 3, 1):
            received[distance] = exchange(pieces[distance - 1], "seq", distance)
        return received[1:]

    key_values = sent(split_heads(place, arrays[1], arrays[2]))
    query_grads = sent(split_heads(place, arrays[0], arrays[3]))
    inputs = gathered_inputs(layer_input[0], me, parity, core, groups)
    halves = []
    if groups > 1:
        mine = [lax.dynamic_slice_in_dim(a, me * HEAD_DIM, HEAD_DIM, 1) for a in arrays[1:3]]
        by_distance = jnp.stack([jnp.stack(mine), *key_values])
        rows = jnp.stack(
            [
                lax.dynamic_index_in_dim(by_distance, me ^ block, 0, keepdims=False)
                for block in range(HEADS)
            ]
        )
        rows = rows.transpose(1, 0, 2, 3).reshape(2, HEADS * tok, HEAD_DIM)
        ahead = [(source, source + HEADS) for source in range(seq_count - HEADS)]
        back = [(source + HEADS, source) for source in range(seq_count - HEADS)]
        halves = [
            lax.ppermute(rows[:, -HALF:], "seq", ahead),
            lax.ppermute(rows[:, :HALF], "seq", back),
        ]
    query_grads[5:], inputs = lax.optimization_barrier((query_grads[5:], inputs))
    grads = head_grads(place, arrays, key_values, query_grads, halves, groups)
    if groups > 1:
        from_after = lax.ppermute(grads[:HALF].astype(jnp.bfloat16), "seq", back)
        from_before = lax.ppermute(grads[-HALF:].astype(jnp.bfloat16), "seq", ahead)
        inner = grads[HALF:-HALF]
        inner = inner.at[-HALF:].add(from_after.astype(jnp.float32))
        inner = inner.at[:HALF].add(from_before.astype(jnp.float32))
        inner = inner.astype(jnp.bfloat16)
        grads = [
            lax.dynamic_slice_in_dim(inner, ((me // 2) ^ distance) * 2 * tok, 2 * tok, 0)
            for distance in range(HEADS // 2)
        ]

    near = [grads[0]] + [None] * (HEADS // 2 - 1)
    for distance in (3, 2, 1):
        near[distance] = exchange(grads[distance], "seq", 2 * distance)
    near_other = [exchange(piece, "dp", 1) for piece in near]
    far = [exchange(piece, "seq", 1) for piece in near]

    if groups > 1:
        far_other = [exchange(piece, "dp", 1) for piece in far]
        members = [list(range(first, seq_count, 2)) for first in (0, 1)]

        def scattered(own, other):
            parts = weight_parts(place, inputs, own, other, jnp.float32)[:-1]
            return lax.psum_scatter(
                jnp.concatenate(parts), "seq", scatter_dimension=0,
                axis_index_groups=members, tiled=True,
            )

        first = scattered(near, near_other)
        second = scattered(far, far_other)
        share, width = first.shape
        shape = (share, HEADS // 2, HEAD_DIM)
        result = ordered(parity, first.reshape(shape), second.reshape(shape), 2)
        return result.reshape(share, 2 * width)

    def spread(parts, total):
        return [total] + [
            exchange(parts[distance], "seq", 2 * distance) for distance in (3, 2, 1)
        ]

    *parts, total = weight_parts(place, inputs, near, near_other, jnp.bfloat16)
    far[2:], parts = lax.optimization_barrier((far[2:], parts))
    first = spread(parts, total)
    far_other = [exchange(piece, "dp", 1) for piece in far]
    *parts, total = weight_parts(place, inputs, far, far_other, jnp.bfloat16)
    return summed(place, first, spread(parts, total))


def solution(mesh):
    spec = P(("parts", "dp"), "seq", None)
    out_specs = P(("parts", "seq", "dp"), None)
    return jax.shard_map(
        local, mesh=mesh, in_specs=(spec,) * 5, out_specs=out_specs, check_vma=False
    )
```

```python
import functools
import math

import jax
import jax.numpy as jnp
from jax import lax
from jax.experimental import pallas as pl
from jax.experimental.pallas import tpu as pltpu
from jax.sharding import PartitionSpec as P

HEADS = 8
HEAD_DIM = 128
HALF = 1024
NEG = -1e30
CHUNK = 2
NT = (((1,), (1,)), ((), ()))


def exchange(value, axis, distance):
    count = lax.axis_size(axis)
    return lax.ppermute(value, axis, [(source, source ^ distance) for source in range(count)])


def fold_rows(value, op):
    rows = value.shape[0]
    total = value[0:8]
    for start in range(8, rows, 8):
        total = op(total, value[start : start + 8])
    return total


def columns(array, block):
    return array[:, pl.ds(pl.multiple_of(block * HEAD_DIM, HEAD_DIM), HEAD_DIM)]


def split_kernel(distances, place, left, right, *outs):
    for distance, out in zip(distances, outs):
        for index, array in enumerate((left, right)):
            out[index] = columns(array, place[0] ^ distance)


def split_heads(place, left, right, distances):
    vmem = pl.BlockSpec(memory_space=pltpu.VMEM)
    tok = left.shape[0]
    shape = jax.ShapeDtypeStruct((2, tok, HEAD_DIM), left.dtype)
    pieces = pl.pallas_call(
        functools.partial(split_kernel, distances),
        out_shape=[shape] * len(distances),
        in_specs=[pl.BlockSpec(memory_space=pltpu.SMEM), vmem, vmem],
        out_specs=[vmem] * len(distances),
        compiler_params=pltpu.CompilerParams(vmem_limit_bytes=4 * 2**20),
        name="split_heads",
    )(place, left, right)
    return dict(zip(distances, pieces))


def core_kernel(place, inputs, out):
    for device in range(HEADS):
        out[device] = columns(inputs, 2 * device + 1 - place[2])


def neighbour_kernel(place, key, value, inputs, other, out):
    count = HEADS // 2
    out[0] = columns(key, place[0] ^ 1)
    out[1] = columns(value, place[0] ^ 1)
    for column in range(count):
        device = 2 * column + 1 - place[0] % 2
        out[2 + column] = columns(inputs, 2 * device + place[2])
        out[2 + count + column] = other[device]


def turned_kernel(place, inputs, other, received, out):
    count = HEADS // 2
    tok = inputs.shape[0]
    parity, core = place[0] % 2, place[2]

    def put(distance, document, side, block):
        start = pl.multiple_of((2 * document + side) * tok, tok)
        out[distance, :, pl.ds(start, tok)] = block.T

    for distance in range(count):
        column = (place[0] // 2) ^ distance
        device = 2 * column + parity
        put(distance, core, parity, columns(inputs, 2 * device + core))
        put(distance, 1 - core, parity, other[device])
        put(distance, core, 1 - parity, received[2 + column])
        put(distance, 1 - core, 1 - parity, received[2 + count + column])


def moved(kernel, shape, dtype, *operands):
    vmem = pl.BlockSpec(memory_space=pltpu.VMEM)
    return pl.pallas_call(
        kernel,
        out_shape=jax.ShapeDtypeStruct(shape, dtype),
        in_specs=[pl.BlockSpec(memory_space=pltpu.SMEM)] + [vmem] * (len(operands) - 1),
        out_specs=vmem,
        compiler_params=pltpu.CompilerParams(vmem_limit_bytes=6 * 2**20),
        name="moved",
    )(*operands)


def head_block(dims, place, b, query, grad, key_ref, value_ref, score_ref, dprob_ref, total_ref):
    tok, halo, groups = dims
    shift = halo // tok
    reach = HALF // tok
    scale = math.log2(math.e) / math.sqrt(HEAD_DIM)
    row = lax.broadcasted_iota(jnp.int32, (tok, tok), 0)
    col = lax.broadcasted_iota(jnp.int32, (tok, tok), 1)
    if halo:
        first, count, lowest = b + shift - reach, 2 * reach + 1, 0
    else:
        first = max(0, b - reach)
        count = min(HEADS, b + reach + 1) - first
        lowest = b - reach - first
    chunks = [range(start, min(start + CHUNK, count)) for start in range(0, count, CHUNK)]

    def rows_of(chunk):
        start = (first + chunk[0]) * tok
        return pl.ds(pl.multiple_of(start, tok) if halo else start, len(chunk) * tok)

    def held(at):
        return slice(at * tok, (at + 1) * tok)

    top = None
    for chunk in chunks:
        scores = lax.dot_general(
            key_ref[rows_of(chunk)], query, NT, preferred_element_type=jnp.float32
        )
        for at in chunk:
            score = scores[held(at - chunk[0])]
            if at == lowest:
                score = jnp.where(row >= col, score, NEG)
            if at == lowest + 2 * reach:
                score = jnp.where(row <= col, score, NEG)
            if halo:
                inside = (first + at >= shift) | (place[1] > 0)
                inside &= (first + at < shift + HEADS) | (place[1] < groups - 1)
                score = jnp.where(inside, score, NEG)
            score_ref[held(at)] = score
            part = fold_rows(score, jnp.maximum)
            top = part if top is None else jnp.maximum(top, part)
    top = jnp.max(top, axis=0, keepdims=True) * scale
    weight_sum = jnp.zeros((8, tok), jnp.float32)
    delta_sum = jnp.zeros((8, tok), jnp.float32)
    for chunk in chunks:
        dprobs = lax.dot_general(
            value_ref[rows_of(chunk)], grad, NT, preferred_element_type=jnp.float32
        )
        for at in chunk:
            dprob = dprobs[held(at - chunk[0])]
            weight = jnp.exp2(score_ref[held(at)] * scale - top)
            score_ref[held(at)] = weight
            dprob_ref[held(at)] = dprob
            weight_sum = weight_sum + fold_rows(weight, jnp.add)
            delta_sum = delta_sum + fold_rows(weight * dprob, jnp.add)
    inverse = 1.0 / jnp.sum(weight_sum, axis=0, keepdims=True)
    delta = jnp.sum(delta_sum, axis=0, keepdims=True) * inverse
    for chunk in chunks:
        held_rows = slice(chunk[0] * tok, (chunk[-1] + 1) * tok)
        prob = score_ref[held_rows] * inverse
        dscore = prob * (dprob_ref[held_rows] - delta)
        total_ref[rows_of(chunk)] += jnp.dot(
            dscore.astype(jnp.bfloat16), query, preferred_element_type=jnp.float32
        )


def query_blocks(dims, place, distances, sources, refs):
    tok = dims[0]
    me = place[0]
    key_ref, value_ref, query_ref, grad_ref, score_ref, dprob_ref, total_ref, sem = refs
    copies = []
    for slot, source in enumerate(sources):
        rows = slice(slot * tok, (slot + 1) * tok)
        for target, piece in zip((query_ref, grad_ref), source):
            copies.append(pltpu.make_async_copy(piece, target.at[rows], sem))
    for copy in copies:
        copy.start()
    yield
    for copy in copies:
        copy.wait()

    def block(at, b, half):
        slot = 2 * at + ((me % 2) ^ half)
        rows = pl.ds(pl.multiple_of(slot * tok, tok), tok)
        head_block(
            dims, place, b, query_ref[rows], grad_ref[rows], key_ref, value_ref,
            score_ref.at[half], dprob_ref.at[half], total_ref,
        )

    for at, distance in enumerate(distances):
        pair = (me // 2) ^ distance
        if dims[1]:

            @pl.loop(0, 2)
            def _(half, at=at, pair=pair):
                block(at, 2 * pair + half, half)

            continue
        for index in range(HEADS // 2):

            @pl.when(pair == index)
            def _(at=at, index=index):
                for half in range(2):
                    block(at, 2 * index + half, half)

    yield


def first_kernel(dims, distances, place, *refs):
    tok, halo, _ = dims
    me = place[0]
    query, key, value, grad = refs[:4]
    key_values, refs = refs[4 : 3 + HEADS], refs[3 + HEADS :]
    count = 2 * len(distances) - 1
    others, refs = refs[:count], refs[count:]
    if halo:
        halves, refs = refs[:2], refs[2:]
    total_ref, key_ref, value_ref, query_ref, grad_ref, score_ref, dprob_ref, sem = refs
    mine = pl.ds(pl.multiple_of(me * HEAD_DIM, HEAD_DIM), HEAD_DIM)
    copies = []
    for distance in range(HEADS):
        rows = pl.ds(pl.multiple_of((me ^ distance) * tok + halo, tok), tok)
        pair = (key, value)
        if distance:
            pair = [key_values[distance - 1].at[index] for index in range(2)]
        else:
            pair = (key.at[:, mine], value.at[:, mine])
        for source, target in zip(pair, (key_ref, value_ref)):
            copies.append(pltpu.make_async_copy(source, target.at[rows], sem))
    if halo:
        for side, start in ((0, 0), (1, halo + HEADS * tok)):
            for index, target in enumerate((key_ref, value_ref)):
                copies.append(
                    pltpu.make_async_copy(
                        halves[side].at[index], target.at[pl.ds(start, halo)], sem
                    )
                )
    for copy in copies:
        copy.start()
    sources = [(query.at[:, mine], grad.at[:, mine])]
    sources += [(other.at[0], other.at[1]) for other in others]
    steps = query_blocks(
        dims, place, distances, sources,
        (key_ref, value_ref, query_ref, grad_ref, score_ref, dprob_ref, total_ref, sem),
    )
    next(steps)
    total_ref[...] = jnp.zeros_like(total_ref)
    for copy in copies:
        copy.wait()
    next(steps)


def later_kernel(dims, distances, last, place, before_ref, key_ref, value_ref, *refs):
    tok, halo, _ = dims
    count = 2 * len(distances)
    others, refs = refs[:count], refs[count:]
    split = last and not halo
    if split:
        outs, refs = refs[: HEADS // 2], refs[HEADS // 2 :]
        total_ref, refs = refs[0], refs[1:]
    else:
        total_ref, refs = refs[0], refs[1:]
    sources = [(other.at[0], other.at[1]) for other in others]
    query_ref, grad_ref, score_ref, dprob_ref, sem = refs
    steps = query_blocks(
        dims, place, distances, sources,
        (key_ref, value_ref, query_ref, grad_ref, score_ref, dprob_ref, total_ref, sem),
    )
    next(steps)
    total_ref[...] = before_ref[...]
    next(steps)
    inverse_root = 1.0 / math.sqrt(HEAD_DIM)
    if split:
        pair = 2 * tok
        for distance, out in enumerate(outs):
            start = pl.multiple_of(((place[0] // 2) ^ distance) * pair, pair)
            out[...] = (total_ref[pl.ds(start, pair)] * inverse_root).astype(jnp.bfloat16)
    elif last:
        total_ref[...] = total_ref[...] * inverse_root


def head_grads(place, arrays, key_values, query_grads, halves, groups):
    tok = arrays[0].shape[0]
    halo = HALF if halves else 0
    dims = (tok, halo, groups)
    span = HEADS * tok + 2 * halo
    window = min(span, tok + 2 * HALF)
    any_spec = pl.BlockSpec(memory_space=pltpu.HBM)
    vmem = pl.BlockSpec(memory_space=pltpu.VMEM)
    smem = pl.BlockSpec(memory_space=pltpu.SMEM)
    total = jax.ShapeDtypeStruct((span, HEAD_DIM), jnp.float32)
    low = jax.ShapeDtypeStruct((span, HEAD_DIM), jnp.bfloat16)
    piece = jax.ShapeDtypeStruct((2 * tok, HEAD_DIM), jnp.bfloat16)
    params = pltpu.CompilerParams(vmem_limit_bytes=(20 if halo else 14) * 2**20)

    def scratch(pairs):
        return [
            pltpu.VMEM((2 * pairs * tok, HEAD_DIM), jnp.bfloat16),
            pltpu.VMEM((2 * pairs * tok, HEAD_DIM), jnp.bfloat16),
            pltpu.VMEM((2, window, tok), jnp.float32),
            pltpu.VMEM((2, window, tok), jnp.float32),
        ]

    def cost(pairs):
        return pl.CostEstimate(
            flops=12 * pairs * tok * window * HEAD_DIM,
            bytes_accessed=8 * span * HEAD_DIM,
            transcendentals=2 * pairs * tok * window,
        )

    sem = [pltpu.SemaphoreType.DMA]
    state = pl.pallas_call(
        functools.partial(first_kernel, dims, (0, 1)),
        out_shape=[total, low, low],
        in_specs=[smem] + [any_spec] * (4 + HEADS - 1 + 3 + len(halves)),
        out_specs=[vmem] * 3,
        scratch_shapes=scratch(2) + sem,
        compiler_params=params,
        cost_estimate=cost(2),
        name="head_first",
    )(place, *arrays, *key_values, *query_grads[:3], *halves)
    for distance in (2, 3):
        last = distance == 3
        split = last and not halo
        others = query_grads[2 * distance - 1 : 2 * distance + 1]
        out = pl.pallas_call(
            functools.partial(later_kernel, dims, (distance,), last),
            out_shape=[piece] * (HEADS // 2) if split else [total],
            in_specs=[smem] + [vmem] * 3 + [any_spec] * 2,
            out_specs=[vmem] * (HEADS // 2 if split else 1),
            scratch_shapes=([pltpu.VMEM(total.shape, total.dtype)] if split else [])
            + scratch(1)
            + sem,
            compiler_params=params,
            cost_estimate=cost(1),
            name="head_later",
        )(place, *state, *others)
        state = [out[0], *state[1:]]
    return out if split else out[0]


def weight_kernel(place, input_ref, *refs):
    count = HEADS // 2
    own, other = refs[0:count], refs[count : 2 * count]
    near_ref, grad_ref = refs[-2:]
    out_refs = refs[2 * count : -2]
    column = place[0] // 2
    core = place[2]
    tokens = own[0].shape[0]
    for distance in range(count):
        start = pl.multiple_of((column ^ distance) * HEAD_DIM, HEAD_DIM)
        at = pl.multiple_of(core * tokens, tokens)
        grad_ref[pl.ds(at, tokens), pl.ds(start, HEAD_DIM)] = own[distance][...]
        at = pl.multiple_of((1 - core) * tokens, tokens)
        grad_ref[pl.ds(at, tokens), pl.ds(start, HEAD_DIM)] = other[distance][...]
    for target in range(input_ref.shape[0]):
        product = jnp.dot(
            input_ref[target], grad_ref[...], preferred_element_type=jnp.float32
        )
        out_refs[target][...] = product.astype(out_refs[target].dtype)
        if target == 0:
            near_ref[...] = product


def weight_parts(place, inputs, own, other, dtype):
    targets, share, depth = inputs.shape
    width = len(own) * HEAD_DIM
    vmem = pl.BlockSpec(memory_space=pltpu.VMEM)
    return pl.pallas_call(
        weight_kernel,
        out_shape=[jax.ShapeDtypeStruct((share, width), dtype)] * targets
        + [jax.ShapeDtypeStruct((share, width), jnp.float32)],
        in_specs=[pl.BlockSpec(memory_space=pltpu.SMEM)] + [vmem] * (1 + len(own) + len(other)),
        out_specs=[vmem] * (targets + 1),
        scratch_shapes=[pltpu.VMEM((depth, width), jnp.bfloat16)],
        compiler_params=pltpu.CompilerParams(vmem_limit_bytes=8 * 2**20),
        cost_estimate=pl.CostEstimate(
            flops=2 * targets * share * depth * width,
            bytes_accessed=2 * depth * (width + targets * share),
            transcendentals=0,
        ),
        name="weight_parts",
    )(place, inputs, *own, *other)


def sum_kernel(place, *refs):
    out_ref = refs[-1]
    count = HEADS // 2
    for side in range(2):
        total = refs[side * count][...]
        for index in range(1, count):
            total = total + refs[side * count + index][...].astype(jnp.float32)
        parity = (place[0] % 2) ^ side
        for column in range(count):
            start = pl.multiple_of((2 * column + parity) * HEAD_DIM, HEAD_DIM)
            out_ref[:, pl.ds(start, HEAD_DIM)] = total[
                :, column * HEAD_DIM : (column + 1) * HEAD_DIM
            ]


def summed(place, near, far):
    share, width = near[0].shape
    vmem = pl.BlockSpec(memory_space=pltpu.VMEM)
    return pl.pallas_call(
        sum_kernel,
        out_shape=jax.ShapeDtypeStruct((share, 2 * width), jnp.float32),
        in_specs=[pl.BlockSpec(memory_space=pltpu.SMEM)] + [vmem] * (len(near) + len(far)),
        out_specs=vmem,
        compiler_params=pltpu.CompilerParams(vmem_limit_bytes=4 * 2**20),
        name="summed",
    )(place, *near, *far)


def ordered(first, own, other, axis):
    return jnp.where(first == 0, jnp.stack([own, other], axis), jnp.stack([other, own], axis))


def gathered_inputs(layer_input, me, parity, core, groups):
    tok, width = layer_input.shape
    columns = lax.axis_size("seq") // 2
    share = width // (columns * 4)
    shaped = layer_input.reshape(tok, columns, 2, 2, share)
    keep = lax.dynamic_index_in_dim(shaped, parity, 2, keepdims=False)
    give = lax.dynamic_index_in_dim(shaped, 1 - parity, 2, keepdims=False)
    both = ordered(parity, keep, exchange(give, "seq", 1), 0)
    both = both.reshape(2 * tok, columns, 2, share)
    keep = lax.dynamic_index_in_dim(both, core, 2, keepdims=False)
    give = lax.dynamic_index_in_dim(both, 1 - core, 2, keepdims=False)
    full = ordered(core, keep, exchange(give, "dp", 1), 0)
    full = full.reshape(4 * tok, columns, share).transpose(1, 2, 0)
    if groups == 1:
        here = me // 2
        full = jnp.stack(
            [
                lax.dynamic_index_in_dim(full, here ^ distance, 0, keepdims=False)
                for distance in range(columns)
            ]
        )
    return full


def after(*values):
    return lax.optimization_barrier(values)


def local(queries, key_states, value_states, out_grad, layer_input):
    seq_count = lax.axis_size("seq")
    groups = seq_count // HEADS
    tok = queries.shape[1]
    index = lax.axis_index("seq")
    core = lax.axis_index("dp")
    me = index % HEADS
    group = index // HEADS
    parity = index % 2
    place = jnp.stack([me, group, core]).astype(jnp.int32)
    arrays = [array[0] for array in (queries, key_states, value_states, out_grad)]

    def sent(pieces, distances):
        return {d: exchange(pieces[d], "seq", d) for d in distances}

    keys, values = arrays[1:3]
    source = layer_input[0]
    width = source.shape[1]
    direct = groups == 1 and width == HEADS * 2 * HEAD_DIM
    if direct:
        apart = (6, 7, 4, 5, 2, 3)
        pieces = split_heads(place, keys, values, apart)
        pieces, source, arrays[0], arrays[3] = after(pieces, source, arrays[0], arrays[3])
        key_values = sent(pieces, apart)
        block = (HEADS, tok, HEAD_DIM)
        other = exchange(moved(core_kernel, block, source.dtype, place, source), "dp", 1)
        block = (HEADS + 2, tok, HEAD_DIM)
        near_piece = moved(
            neighbour_kernel, block, source.dtype, place, keys, values, source, other
        )
        key_values[1] = exchange(near_piece, "seq", 1)
        shape = (HEADS // 2, HEAD_DIM, 4 * tok)
        inputs = moved(
            turned_kernel, shape, source.dtype, place, source, other, key_values[1]
        )
    else:
        every = (6, 7, 4, 5, 2, 3, 1)
        key_values = sent(split_heads(place, keys, values, every), every)
        inputs = gathered_inputs(source, me, parity, core, groups)
    every = (4, 5, 2, 3, 1, 6, 7)
    pieces = split_heads(place, arrays[0], arrays[3], every)
    for first, second in ((2, 2), (3, 3), (6, 1), (6, 4), (7, 5), (4, 6), (5, 7)):
        key_values[first], pieces[second] = after(key_values[first], pieces[second])
    query_grads = sent(pieces, every)
    key_values = [key_values[d] for d in range(1, HEADS)]
    query_grads = [query_grads[d] for d in range(1, HEADS)]
    halves = []
    if groups > 1:
        mine = [lax.dynamic_slice_in_dim(a, me * HEAD_DIM, HEAD_DIM, 1) for a in arrays[1:3]]
        by_distance = jnp.stack([jnp.stack(mine), *key_values])
        rows = jnp.stack(
            [
                lax.dynamic_index_in_dim(by_distance, me ^ block, 0, keepdims=False)
                for block in range(HEADS)
            ]
        )
        rows = rows.transpose(1, 0, 2, 3).reshape(2, HEADS * tok, HEAD_DIM)
        ahead = [(source, source + HEADS) for source in range(seq_count - HEADS)]
        back = [(source + HEADS, source) for source in range(seq_count - HEADS)]
        halves = [
            lax.ppermute(rows[:, -HALF:], "seq", ahead),
            lax.ppermute(rows[:, :HALF], "seq", back),
        ]
    query_grads[5:], inputs = after(query_grads[5:], inputs)
    grads = head_grads(place, arrays, key_values, query_grads, halves, groups)
    if groups > 1:
        from_after = lax.ppermute(grads[:HALF].astype(jnp.bfloat16), "seq", back)
        from_before = lax.ppermute(grads[-HALF:].astype(jnp.bfloat16), "seq", ahead)
        inner = grads[HALF:-HALF]
        inner = inner.at[-HALF:].add(from_after.astype(jnp.float32))
        inner = inner.at[:HALF].add(from_before.astype(jnp.float32))
        inner = inner.astype(jnp.bfloat16)
        grads = [
            lax.dynamic_slice_in_dim(inner, ((me // 2) ^ distance) * 2 * tok, 2 * tok, 0)
            for distance in range(HEADS // 2)
        ]

    near = [grads[0]] + [None] * (HEADS // 2 - 1)
    for distance in (3, 2, 1):
        near[distance] = exchange(grads[distance], "seq", 2 * distance)
    near_other = [exchange(piece, "dp", 1) for piece in near]
    far = [exchange(piece, "seq", 1) for piece in near]

    if groups > 1:
        far_other = [exchange(piece, "dp", 1) for piece in far]
        members = [list(range(first, seq_count, 2)) for first in (0, 1)]

        def scattered(own, other):
            parts = weight_parts(place, inputs, own, other, jnp.float32)[:-1]
            return lax.psum_scatter(
                jnp.concatenate(parts), "seq", scatter_dimension=0,
                axis_index_groups=members, tiled=True,
            )

        first = scattered(near, near_other)
        second = scattered(far, far_other)
        share, width = first.shape
        shape = (share, HEADS // 2, HEAD_DIM)
        result = ordered(parity, first.reshape(shape), second.reshape(shape), 2)
        return result.reshape(share, 2 * width)

    def spread(parts, total):
        return [total] + [
            exchange(parts[distance], "seq", 2 * distance) for distance in (3, 2, 1)
        ]

    near_other, far[:2] = after(near_other, far[:2])
    *parts, total = weight_parts(place, inputs, near, near_other, jnp.bfloat16)
    first = spread(parts, total)
    far[2:], first[1] = after(far[2:], first[1])
    far_other = [exchange(piece, "dp", 1) for piece in far]
    *parts, total = weight_parts(place, inputs, far, far_other, jnp.bfloat16)
    return summed(place, first, spread(parts, total))


def solution(mesh):
    spec = P(("parts", "dp"), "seq", None)
    out_specs = P(("parts", "seq", "dp"), None)
    return jax.shard_map(
        local, mesh=mesh, in_specs=(spec,) * 5, out_specs=out_specs, check_vma=False
    )
```

```python
import functools
import math

import jax
import jax.numpy as jnp
from jax import lax
from jax.experimental import pallas as pl
from jax.experimental.pallas import tpu as pltpu
from jax.sharding import PartitionSpec as P

HEADS = 8
HEAD_DIM = 128
HALF = 1024
NEG = -1e30
CHUNK = 2
NT = (((1,), (1,)), ((), ()))


def exchange(value, axis, distance):
    count = lax.axis_size(axis)
    return lax.ppermute(value, axis, [(source, source ^ distance) for source in range(count)])


def fold_rows(value, op):
    rows = value.shape[0]
    total = value[0:8]
    for start in range(8, rows, 8):
        total = op(total, value[start : start + 8])
    return total


def columns(array, block):
    return array[:, pl.ds(pl.multiple_of(block * HEAD_DIM, HEAD_DIM), HEAD_DIM)]


def split_kernel(distances, place, left, right, *outs):
    for distance, out in zip(distances, outs):
        for index, array in enumerate((left, right)):
            out[index] = columns(array, place[0] ^ distance)


def split_heads(place, left, right, distances):
    vmem = pl.BlockSpec(memory_space=pltpu.VMEM)
    tok = left.shape[0]
    shape = jax.ShapeDtypeStruct((2, tok, HEAD_DIM), left.dtype)
    pieces = pl.pallas_call(
        functools.partial(split_kernel, distances),
        out_shape=[shape] * len(distances),
        in_specs=[pl.BlockSpec(memory_space=pltpu.SMEM), vmem, vmem],
        out_specs=[vmem] * len(distances),
        compiler_params=pltpu.CompilerParams(vmem_limit_bytes=4 * 2**20),
        name="split_heads",
    )(place, left, right)
    return dict(zip(distances, pieces))


def core_kernel(place, inputs, out):
    for device in range(HEADS):
        out[device] = columns(inputs, 2 * device + 1 - place[2])


def neighbour_kernel(place, inputs, other, out):
    count = HEADS // 2
    for column in range(count):
        device = 2 * column + 1 - place[0] % 2
        out[column] = columns(inputs, 2 * device + place[2])
        out[count + column] = other[device]


def turned_kernel(place, inputs, other, received, out):
    count = HEADS // 2
    tok = inputs.shape[0]
    parity, core = place[0] % 2, place[2]

    def put(distance, document, side, block):
        start = pl.multiple_of((2 * document + side) * tok, tok)
        out[distance, :, pl.ds(start, tok)] = block.T

    for distance in range(count):
        column = (place[0] // 2) ^ distance
        device = 2 * column + parity
        put(distance, core, parity, columns(inputs, 2 * device + core))
        put(distance, 1 - core, parity, other[device])
        put(distance, core, 1 - parity, received[column])
        put(distance, 1 - core, 1 - parity, received[count + column])


def moved(kernel, shape, dtype, *operands):
    vmem = pl.BlockSpec(memory_space=pltpu.VMEM)
    return pl.pallas_call(
        kernel,
        out_shape=jax.ShapeDtypeStruct(shape, dtype),
        in_specs=[pl.BlockSpec(memory_space=pltpu.SMEM)] + [vmem] * (len(operands) - 1),
        out_specs=vmem,
        compiler_params=pltpu.CompilerParams(vmem_limit_bytes=6 * 2**20),
        name="moved",
    )(*operands)


def head_block(dims, place, b, query, grad, key_ref, value_ref, score_ref, dprob_ref, total_ref):
    tok, halo, groups = dims
    shift = halo // tok
    reach = HALF // tok
    scale = math.log2(math.e) / math.sqrt(HEAD_DIM)
    ahead = lax.broadcasted_iota(jnp.int32, (tok, tok), 0)
    ahead = ahead - lax.broadcasted_iota(jnp.int32, (tok, tok), 1)
    first, count = (b + shift - reach, 2 * reach + 1) if halo else (0, HEADS)
    chunks = [range(start, min(start + CHUNK, count)) for start in range(0, count, CHUNK)]

    def rows_of(chunk):
        start = (first + chunk[0]) * tok
        return pl.ds(pl.multiple_of(start, tok) if halo else start, len(chunk) * tok)

    def held(at):
        return slice(at * tok, (at + 1) * tok)

    top = None
    for chunk in chunks:
        scores = lax.dot_general(
            key_ref[rows_of(chunk)], query, NT, preferred_element_type=jnp.float32
        )
        for at in chunk:
            score = scores[held(at - chunk[0])]
            distance = first + at - shift - b
            if at == 0 if halo else at < HEADS - reach:
                score = jnp.where(ahead >= -HALF - distance * tok, score, NEG)
            if at == 2 * reach if halo else at >= reach:
                score = jnp.where(ahead <= HALF - distance * tok, score, NEG)
            if halo:
                inside = (first + at >= shift) | (place[1] > 0)
                inside &= (first + at < shift + HEADS) | (place[1] < groups - 1)
                score = jnp.where(inside, score, NEG)
            score_ref[held(at)] = score
            part = fold_rows(score, jnp.maximum)
            top = part if top is None else jnp.maximum(top, part)
    top = jnp.max(top, axis=0, keepdims=True) * scale
    weight_sum = jnp.zeros((8, tok), jnp.float32)
    delta_sum = jnp.zeros((8, tok), jnp.float32)
    for chunk in chunks:
        dprobs = lax.dot_general(
            value_ref[rows_of(chunk)], grad, NT, preferred_element_type=jnp.float32
        )
        for at in chunk:
            dprob = dprobs[held(at - chunk[0])]
            weight = jnp.exp2(score_ref[held(at)] * scale - top)
            score_ref[held(at)] = weight
            dprob_ref[held(at)] = dprob
            weight_sum = weight_sum + fold_rows(weight, jnp.add)
            delta_sum = delta_sum + fold_rows(weight * dprob, jnp.add)
    inverse = 1.0 / jnp.sum(weight_sum, axis=0, keepdims=True)
    delta = jnp.sum(delta_sum, axis=0, keepdims=True) * inverse
    for chunk in chunks:
        held_rows = slice(chunk[0] * tok, (chunk[-1] + 1) * tok)
        prob = score_ref[held_rows] * inverse
        dscore = prob * (dprob_ref[held_rows] - delta)
        total_ref[rows_of(chunk)] += jnp.dot(
            dscore.astype(jnp.bfloat16), query, preferred_element_type=jnp.float32
        )


def query_blocks(dims, place, distances, sources, refs):
    tok = dims[0]
    me = place[0]
    key_ref, value_ref, query_ref, grad_ref, score_ref, dprob_ref, total_ref, sem = refs
    copies = []
    for slot, source in enumerate(sources):
        rows = slice(slot * tok, (slot + 1) * tok)
        for target, piece in zip((query_ref, grad_ref), source):
            copies.append(pltpu.make_async_copy(piece, target.at[rows], sem))
    for copy in copies:
        copy.start()
    yield
    for copy in copies:
        copy.wait()

    def block(slot, distance):
        rows = pl.ds(pl.multiple_of(slot * tok, tok), tok)
        head_block(
            dims, place, me ^ distance, query_ref[rows], grad_ref[rows], key_ref, value_ref,
            score_ref, dprob_ref, total_ref,
        )

    @pl.loop(0, 2 * len(distances))
    def _(slot):
        block(slot, 2 * distances[0] + slot)

    yield


def first_kernel(dims, distances, place, *refs):
    tok, halo, _ = dims
    me = place[0]
    query, key, value, grad = refs[:4]
    key_values, refs = refs[4 : 3 + HEADS], refs[3 + HEADS :]
    count = 2 * len(distances) - 1
    others, refs = refs[:count], refs[count:]
    if halo:
        halves, refs = refs[:2], refs[2:]
    total_ref, key_ref, value_ref, query_ref, grad_ref, score_ref, dprob_ref, sem = refs
    mine = pl.ds(pl.multiple_of(me * HEAD_DIM, HEAD_DIM), HEAD_DIM)
    copies = []
    for distance in range(HEADS):
        rows = pl.ds(pl.multiple_of((me ^ distance) * tok + halo, tok), tok)
        pair = (key, value)
        if distance:
            pair = [key_values[distance - 1].at[index] for index in range(2)]
        else:
            pair = (key.at[:, mine], value.at[:, mine])
        for source, target in zip(pair, (key_ref, value_ref)):
            copies.append(pltpu.make_async_copy(source, target.at[rows], sem))
    if halo:
        for side, start in ((0, 0), (1, halo + HEADS * tok)):
            for index, target in enumerate((key_ref, value_ref)):
                copies.append(
                    pltpu.make_async_copy(
                        halves[side].at[index], target.at[pl.ds(start, halo)], sem
                    )
                )
    for copy in copies:
        copy.start()
    sources = [(query.at[:, mine], grad.at[:, mine])]
    sources += [(other.at[0], other.at[1]) for other in others]
    steps = query_blocks(
        dims, place, distances, sources,
        (key_ref, value_ref, query_ref, grad_ref, score_ref, dprob_ref, total_ref, sem),
    )
    next(steps)
    total_ref[...] = jnp.zeros_like(total_ref)
    for copy in copies:
        copy.wait()
    next(steps)


def later_kernel(dims, distances, last, place, before_ref, key_ref, value_ref, *refs):
    tok, halo, _ = dims
    count = 2 * len(distances)
    others, refs = refs[:count], refs[count:]
    split = last and not halo
    if split:
        outs, refs = refs[: HEADS // 2], refs[HEADS // 2 :]
        total_ref, refs = refs[0], refs[1:]
    else:
        total_ref, refs = refs[0], refs[1:]
    sources = [(other.at[0], other.at[1]) for other in others]
    query_ref, grad_ref, score_ref, dprob_ref, sem = refs
    steps = query_blocks(
        dims, place, distances, sources,
        (key_ref, value_ref, query_ref, grad_ref, score_ref, dprob_ref, total_ref, sem),
    )
    next(steps)
    total_ref[...] = before_ref[...]
    next(steps)
    inverse_root = 1.0 / math.sqrt(HEAD_DIM)
    if split:
        pair = 2 * tok
        for distance, out in enumerate(outs):
            start = pl.multiple_of(((place[0] // 2) ^ distance) * pair, pair)
            out[...] = (total_ref[pl.ds(start, pair)] * inverse_root).astype(jnp.bfloat16)
    elif last:
        total_ref[...] = total_ref[...] * inverse_root


def head_grads(place, arrays, key_values, query_grads, halves, groups):
    tok = arrays[0].shape[0]
    halo = HALF if halves else 0
    dims = (tok, halo, groups)
    span = HEADS * tok + 2 * halo
    window = min(span, tok + 2 * HALF)
    any_spec = pl.BlockSpec(memory_space=pltpu.HBM)
    vmem = pl.BlockSpec(memory_space=pltpu.VMEM)
    smem = pl.BlockSpec(memory_space=pltpu.SMEM)
    total = jax.ShapeDtypeStruct((span, HEAD_DIM), jnp.float32)
    low = jax.ShapeDtypeStruct((span, HEAD_DIM), jnp.bfloat16)
    piece = jax.ShapeDtypeStruct((2 * tok, HEAD_DIM), jnp.bfloat16)
    params = pltpu.CompilerParams(vmem_limit_bytes=(14 if halo else 10) * 2**20)

    def scratch(pairs):
        return [
            pltpu.VMEM((2 * pairs * tok, HEAD_DIM), jnp.bfloat16),
            pltpu.VMEM((2 * pairs * tok, HEAD_DIM), jnp.bfloat16),
            pltpu.VMEM((window, tok), jnp.float32),
            pltpu.VMEM((window, tok), jnp.float32),
        ]

    def cost(pairs):
        return pl.CostEstimate(
            flops=100 * pairs * tok * window * HEAD_DIM,
            bytes_accessed=8 * span * HEAD_DIM,
            transcendentals=2 * pairs * tok * window,
        )

    sem = [pltpu.SemaphoreType.DMA]
    state = pl.pallas_call(
        functools.partial(first_kernel, dims, (0, 1)),
        out_shape=[total, low, low],
        in_specs=[smem] + [any_spec] * (4 + HEADS - 1 + 3 + len(halves)),
        out_specs=[vmem] * 3,
        scratch_shapes=scratch(2) + sem,
        compiler_params=params,
        cost_estimate=cost(2),
        name="head_first",
    )(place, *arrays, *key_values, *query_grads[:3], *halves)
    for distance in (2, 3):
        last = distance == 3
        split = last and not halo
        others = query_grads[2 * distance - 1 : 2 * distance + 1]
        out = pl.pallas_call(
            functools.partial(later_kernel, dims, (distance,), last),
            out_shape=[piece] * (HEADS // 2) if split else [total],
            in_specs=[smem] + [vmem] * 3 + [any_spec] * 2,
            out_specs=[vmem] * (HEADS // 2 if split else 1),
            scratch_shapes=([pltpu.VMEM(total.shape, total.dtype)] if split else [])
            + scratch(1)
            + sem,
            compiler_params=params,
            cost_estimate=cost(1),
            name="head_later",
        )(place, *state, *others)
        state = [out[0], *state[1:]]
    return out if split else out[0]


def weight_kernel(place, input_ref, *refs):
    count = HEADS // 2
    own, other = refs[0:count], refs[count : 2 * count]
    near_ref, grad_ref = refs[-2:]
    out_refs = refs[2 * count : -2]
    column = place[0] // 2
    core = place[2]
    tokens = own[0].shape[0]
    for distance in range(count):
        start = pl.multiple_of((column ^ distance) * HEAD_DIM, HEAD_DIM)
        at = pl.multiple_of(core * tokens, tokens)
        grad_ref[pl.ds(at, tokens), pl.ds(start, HEAD_DIM)] = own[distance][...]
        at = pl.multiple_of((1 - core) * tokens, tokens)
        grad_ref[pl.ds(at, tokens), pl.ds(start, HEAD_DIM)] = other[distance][...]
    for target in range(input_ref.shape[0]):
        product = jnp.dot(
            input_ref[target], grad_ref[...], preferred_element_type=jnp.float32
        )
        out_refs[target][...] = product.astype(out_refs[target].dtype)
        if target == 0:
            near_ref[...] = product


def weight_parts(place, inputs, own, other, dtype):
    targets, share, depth = inputs.shape
    width = len(own) * HEAD_DIM
    vmem = pl.BlockSpec(memory_space=pltpu.VMEM)
    return pl.pallas_call(
        weight_kernel,
        out_shape=[jax.ShapeDtypeStruct((share, width), dtype)] * targets
        + [jax.ShapeDtypeStruct((share, width), jnp.float32)],
        in_specs=[pl.BlockSpec(memory_space=pltpu.SMEM)] + [vmem] * (1 + len(own) + len(other)),
        out_specs=[vmem] * (targets + 1),
        scratch_shapes=[pltpu.VMEM((depth, width), jnp.bfloat16)],
        compiler_params=pltpu.CompilerParams(vmem_limit_bytes=8 * 2**20),
        cost_estimate=pl.CostEstimate(
            flops=2 * targets * share * depth * width,
            bytes_accessed=2 * depth * (width + targets * share),
            transcendentals=0,
        ),
        name="weight_parts",
    )(place, inputs, *own, *other)


def sum_kernel(place, *refs):
    out_ref = refs[-1]
    count = HEADS // 2
    for side in range(2):
        total = refs[side * count][...]
        for index in range(1, count):
            total = total + refs[side * count + index][...].astype(jnp.float32)
        parity = (place[0] % 2) ^ side
        for column in range(count):
            start = pl.multiple_of((2 * column + parity) * HEAD_DIM, HEAD_DIM)
            out_ref[:, pl.ds(start, HEAD_DIM)] = total[
                :, column * HEAD_DIM : (column + 1) * HEAD_DIM
            ]


def summed(place, near, far):
    share, width = near[0].shape
    vmem = pl.BlockSpec(memory_space=pltpu.VMEM)
    return pl.pallas_call(
        sum_kernel,
        out_shape=jax.ShapeDtypeStruct((share, 2 * width), jnp.float32),
        in_specs=[pl.BlockSpec(memory_space=pltpu.SMEM)] + [vmem] * (len(near) + len(far)),
        out_specs=vmem,
        compiler_params=pltpu.CompilerParams(vmem_limit_bytes=4 * 2**20),
        name="summed",
    )(place, *near, *far)


def ordered(first, own, other, axis):
    return jnp.where(first == 0, jnp.stack([own, other], axis), jnp.stack([other, own], axis))


def gathered_inputs(layer_input, me, parity, core, groups):
    tok, width = layer_input.shape
    columns = lax.axis_size("seq") // 2
    share = width // (columns * 4)
    shaped = layer_input.reshape(tok, columns, 2, 2, share)
    keep = lax.dynamic_index_in_dim(shaped, parity, 2, keepdims=False)
    give = lax.dynamic_index_in_dim(shaped, 1 - parity, 2, keepdims=False)
    both = ordered(parity, keep, exchange(give, "seq", 1), 0)
    both = both.reshape(2 * tok, columns, 2, share)
    keep = lax.dynamic_index_in_dim(both, core, 2, keepdims=False)
    give = lax.dynamic_index_in_dim(both, 1 - core, 2, keepdims=False)
    full = ordered(core, keep, exchange(give, "dp", 1), 0)
    full = full.reshape(4 * tok, columns, share).transpose(1, 2, 0)
    if groups == 1:
        here = me // 2
        full = jnp.stack(
            [
                lax.dynamic_index_in_dim(full, here ^ distance, 0, keepdims=False)
                for distance in range(columns)
            ]
        )
    return full


def after(*values):
    return lax.optimization_barrier(values)


def local(queries, key_states, value_states, out_grad, layer_input):
    seq_count = lax.axis_size("seq")
    groups = seq_count // HEADS
    tok = queries.shape[1]
    index = lax.axis_index("seq")
    core = lax.axis_index("dp")
    me = index % HEADS
    group = index // HEADS
    parity = index % 2
    place = jnp.stack([me, group, core]).astype(jnp.int32)
    arrays = [array[0] for array in (queries, key_states, value_states, out_grad)]

    def sent(pieces, distances):
        return {d: exchange(pieces[d], "seq", d) for d in distances}

    keys, values = arrays[1:3]
    source = layer_input[0]
    width = source.shape[1]
    every = (6, 7, 4, 5, 2, 3, 1)
    direct = groups == 1 and width == HEADS * 2 * HEAD_DIM
    if direct:
        pieces = split_heads(place, keys, values, every)
        key_values = sent(pieces, (6, 7, 1, 2, 3))
        for first, second in ((6, 4), (7, 5)):
            key_values[first], pieces[second] = after(key_values[first], pieces[second])
        key_values |= sent(pieces, (4, 5))
        key_values[1], source = after(key_values[1], source)
        block = (HEADS, tok, HEAD_DIM)
        other = exchange(moved(core_kernel, block, source.dtype, place, source), "dp", 1)
        near_piece = moved(neighbour_kernel, block, source.dtype, place, source, other)
        received = exchange(near_piece, "seq", 1)
        shape = (HEADS // 2, HEAD_DIM, 4 * tok)
        inputs = moved(turned_kernel, shape, source.dtype, place, source, other, received)
    else:
        key_values = sent(split_heads(place, keys, values, every), every)
        inputs = gathered_inputs(source, me, parity, core, groups)
    pieces = split_heads(place, arrays[0], arrays[3], every)
    for first, second in ((1, 1), (2, 2), (3, 3), (4, 4), (5, 5), (5, 6)):
        key_values[first], pieces[second] = after(key_values[first], pieces[second])
    query_grads = sent(pieces, (1, 2, 3, 4, 5, 6))
    query_grads[4], pieces[7] = after(query_grads[4], pieces[7])
    query_grads[7] = exchange(pieces[7], "seq", 7)
    key_values = [key_values[d] for d in range(1, HEADS)]
    query_grads = [query_grads[d] for d in range(1, HEADS)]
    halves = []
    if groups > 1:
        mine = [lax.dynamic_slice_in_dim(a, me * HEAD_DIM, HEAD_DIM, 1) for a in arrays[1:3]]
        by_distance = jnp.stack([jnp.stack(mine), *key_values])
        rows = jnp.stack(
            [
                lax.dynamic_index_in_dim(by_distance, me ^ block, 0, keepdims=False)
                for block in range(HEADS)
            ]
        )
        rows = rows.transpose(1, 0, 2, 3).reshape(2, HEADS * tok, HEAD_DIM)
        ahead = [(source, source + HEADS) for source in range(seq_count - HEADS)]
        back = [(source + HEADS, source) for source in range(seq_count - HEADS)]
        halves = [
            lax.ppermute(rows[:, -HALF:], "seq", ahead),
            lax.ppermute(rows[:, :HALF], "seq", back),
        ]
    grads = head_grads(place, arrays, key_values, query_grads, halves, groups)
    if groups > 1:
        from_after = lax.ppermute(grads[:HALF].astype(jnp.bfloat16), "seq", back)
        from_before = lax.ppermute(grads[-HALF:].astype(jnp.bfloat16), "seq", ahead)
        inner = grads[HALF:-HALF]
        inner = inner.at[-HALF:].add(from_after.astype(jnp.float32))
        inner = inner.at[:HALF].add(from_before.astype(jnp.float32))
        inner = inner.astype(jnp.bfloat16)
        grads = [
            lax.dynamic_slice_in_dim(inner, ((me // 2) ^ distance) * 2 * tok, 2 * tok, 0)
            for distance in range(HEADS // 2)
        ]

    near = [grads[0]] + [None] * (HEADS // 2 - 1)
    for distance in (3, 2, 1):
        near[distance] = exchange(grads[distance], "seq", 2 * distance)
    near_other = [exchange(piece, "dp", 1) for piece in near]
    far = [exchange(piece, "seq", 1) for piece in near]

    if groups > 1:
        far_other = [exchange(piece, "dp", 1) for piece in far]
        members = [list(range(first, seq_count, 2)) for first in (0, 1)]

        def scattered(own, other):
            parts = weight_parts(place, inputs, own, other, jnp.float32)[:-1]
            return lax.psum_scatter(
                jnp.concatenate(parts), "seq", scatter_dimension=0,
                axis_index_groups=members, tiled=True,
            )

        first = scattered(near, near_other)
        second = scattered(far, far_other)
        share, width = first.shape
        shape = (share, HEADS // 2, HEAD_DIM)
        result = ordered(parity, first.reshape(shape), second.reshape(shape), 2)
        return result.reshape(share, 2 * width)

    def spread(parts, total):
        return [total] + [
            exchange(parts[distance], "seq", 2 * distance) for distance in (3, 2, 1)
        ]

    near_other, far[:2] = after(near_other, far[:2])
    *parts, total = weight_parts(place, inputs, near, near_other, jnp.bfloat16)
    first = spread(parts, total)
    far[2:], first[1] = after(far[2:], first[1])
    far_other = [exchange(piece, "dp", 1) for piece in far]
    *parts, total = weight_parts(place, inputs, far, far_other, jnp.bfloat16)
    return summed(place, first, spread(parts, total))


def solution(mesh):
    spec = P(("parts", "dp"), "seq", None)
    out_specs = P(("parts", "seq", "dp"), None)
    return jax.shard_map(
        local, mesh=mesh, in_specs=(spec,) * 5, out_specs=out_specs, check_vma=False
    )
```

```python
import functools
import math

import jax
import jax.numpy as jnp
from jax import lax
from jax.experimental import pallas as pl
from jax.experimental.pallas import tpu as pltpu
from jax.sharding import PartitionSpec as P

HEADS = 8
HEAD_DIM = 128
HALF = 1024
NEG = -1e30
CHUNK = 2
NT = (((1,), (1,)), ((), ()))


def exchange(value, axis, distance):
    count = lax.axis_size(axis)
    return lax.ppermute(value, axis, [(source, source ^ distance) for source in range(count)])


def fold_rows(value, op):
    rows = value.shape[0]
    total = value[0:8]
    for start in range(8, rows, 8):
        total = op(total, value[start : start + 8])
    return total


def slot_distances(column, core):
    aside = (column % 2) ^ core
    return (2 + aside, 3 - aside, 1 - aside, aside)


def slot_route(slot):
    pairs = []
    for source in range(lax.axis_size("seq")):
        for core in range(2):
            column, parity = source // 2, source % 2
            target = column ^ slot_distances(column, core)[slot]
            pairs.append((2 * source + core, 2 * (2 * target + parity) + column % 2))
    return pairs


def columns(array, block):
    return array[:, pl.ds(pl.multiple_of(block * HEAD_DIM, HEAD_DIM), HEAD_DIM)]


def split_kernel(distances, place, left, right, *refs):
    outs, sem = refs[:-1], refs[-1]
    copies = []
    for distance, out in zip(distances, outs):
        start = pl.multiple_of((place[0] ^ distance) * HEAD_DIM, HEAD_DIM)
        for index, array in enumerate((left, right)):
            piece = array.at[:, pl.ds(start, HEAD_DIM)]
            copies.append(pltpu.make_async_copy(piece, out.at[index], sem))
    for copy in copies:
        copy.start()
    for copy in copies:
        copy.wait()


def split_heads(place, left, right, distances):
    vmem = pl.BlockSpec(memory_space=pltpu.VMEM)
    hbm = pl.BlockSpec(memory_space=pltpu.HBM)
    tok = left.shape[0]
    shape = jax.ShapeDtypeStruct((2, tok, HEAD_DIM), left.dtype)
    pieces = pl.pallas_call(
        functools.partial(split_kernel, distances),
        out_shape=[shape] * len(distances),
        in_specs=[pl.BlockSpec(memory_space=pltpu.SMEM), hbm, hbm],
        out_specs=[vmem] * len(distances),
        scratch_shapes=[pltpu.SemaphoreType.DMA],
        compiler_params=pltpu.CompilerParams(vmem_limit_bytes=4 * 2**20),
        name="split_heads",
    )(place, left, right)
    return dict(zip(distances, pieces))


def sides_kernel(place, inputs, keep, give):
    for column in range(HEADS // 2):
        for core in range(2):
            device = 2 * column + place[0] % 2
            keep[2 * column + core] = columns(inputs, 2 * device + core)
            device = 2 * column + 1 - place[0] % 2
            give[2 * column + core] = columns(inputs, 2 * device + core)


def turned_kernel(place, keep, keep_other, received, received_other, out):
    tok = keep.shape[1]
    parity, core = place[0] % 2, place[2]
    for distance in range(HEADS // 2):
        for target in range(2):
            index = 2 * ((place[0] // 2) ^ distance) + target
            rows = slice(target * HEAD_DIM, (target + 1) * HEAD_DIM)
            for document, side, blocks in (
                (core, parity, keep),
                (1 - core, parity, keep_other),
                (core, 1 - parity, received),
                (1 - core, 1 - parity, received_other),
            ):
                start = pl.multiple_of((2 * document + side) * tok, tok)
                out[distance, rows, pl.ds(start, tok)] = blocks[index].T


def moved(kernel, shapes, *operands):
    vmem = pl.BlockSpec(memory_space=pltpu.VMEM)
    return pl.pallas_call(
        kernel,
        out_shape=shapes,
        in_specs=[pl.BlockSpec(memory_space=pltpu.SMEM)] + [vmem] * (len(operands) - 1),
        out_specs=[vmem] * len(shapes),
        compiler_params=pltpu.CompilerParams(vmem_limit_bytes=6 * 2**20),
        name="moved",
    )(*operands)


def head_block(dims, place, b, query, grad, key_ref, value_ref, score_ref, dprob_ref, total_ref):
    tok, halo, groups = dims
    shift = halo // tok
    reach = HALF // tok
    scale = math.log2(math.e) / math.sqrt(HEAD_DIM)
    ahead = lax.broadcasted_iota(jnp.int32, (tok, tok), 0)
    ahead = ahead - lax.broadcasted_iota(jnp.int32, (tok, tok), 1)
    first, count = (b + shift - reach, 2 * reach + 1) if halo else (0, HEADS)
    chunks = [range(start, min(start + CHUNK, count)) for start in range(0, count, CHUNK)]

    def rows_of(chunk):
        start = (first + chunk[0]) * tok
        return pl.ds(pl.multiple_of(start, tok) if halo else start, len(chunk) * tok)

    def held(at):
        return slice(at * tok, (at + 1) * tok)

    top = None
    for chunk in chunks:
        scores = lax.dot_general(
            key_ref[rows_of(chunk)], query, NT, preferred_element_type=jnp.float32
        )
        for at in chunk:
            score = scores[held(at - chunk[0])]
            distance = first + at - shift - b
            if at == 0 if halo else at < HEADS - reach:
                score = jnp.where(ahead >= -HALF - distance * tok, score, NEG)
            if at == 2 * reach if halo else at >= reach:
                score = jnp.where(ahead <= HALF - distance * tok, score, NEG)
            if halo:
                inside = (first + at >= shift) | (place[1] > 0)
                inside &= (first + at < shift + HEADS) | (place[1] < groups - 1)
                score = jnp.where(inside, score, NEG)
            score_ref[held(at)] = score
            part = fold_rows(score, jnp.maximum)
            top = part if top is None else jnp.maximum(top, part)
    top = jnp.max(top, axis=0, keepdims=True) * scale
    weight_sum = jnp.zeros((8, tok), jnp.float32)
    delta_sum = jnp.zeros((8, tok), jnp.float32)
    for chunk in chunks:
        dprobs = lax.dot_general(
            value_ref[rows_of(chunk)], grad, NT, preferred_element_type=jnp.float32
        )
        for at in chunk:
            dprob = dprobs[held(at - chunk[0])]
            weight = jnp.exp2(score_ref[held(at)] * scale - top)
            score_ref[held(at)] = weight
            dprob_ref[held(at)] = dprob
            weight_sum = weight_sum + fold_rows(weight, jnp.add)
            delta_sum = delta_sum + fold_rows(weight * dprob, jnp.add)
    inverse = 1.0 / jnp.sum(weight_sum, axis=0, keepdims=True)
    delta = jnp.sum(delta_sum, axis=0, keepdims=True) * inverse
    for chunk in chunks:
        held_rows = slice(chunk[0] * tok, (chunk[-1] + 1) * tok)
        prob = score_ref[held_rows] * inverse
        dscore = prob * (dprob_ref[held_rows] - delta)
        total_ref[rows_of(chunk)] += jnp.dot(
            dscore.astype(jnp.bfloat16), query, preferred_element_type=jnp.float32
        )


def query_blocks(dims, place, distances, sources, refs):
    tok = dims[0]
    me = place[0]
    key_ref, value_ref, query_ref, grad_ref, score_ref, dprob_ref, total_ref, sem = refs
    copies = []
    for slot, source in enumerate(sources):
        rows = slice(slot * tok, (slot + 1) * tok)
        for target, piece in zip((query_ref, grad_ref), source):
            copies.append(pltpu.make_async_copy(piece, target.at[rows], sem))
    for copy in copies:
        copy.start()
    yield
    for copy in copies:
        copy.wait()

    def block(slot, distance):
        rows = pl.ds(pl.multiple_of(slot * tok, tok), tok)
        head_block(
            dims, place, me ^ distance, query_ref[rows], grad_ref[rows], key_ref, value_ref,
            score_ref, dprob_ref, total_ref,
        )

    @pl.loop(0, 2 * len(distances))
    def _(slot):
        block(slot, 2 * distances[0] + slot)

    yield


def first_kernel(dims, distances, place, *refs):
    tok, halo, _ = dims
    me = place[0]
    query, key, value, grad = refs[:4]
    key_values, refs = refs[4 : 3 + HEADS], refs[3 + HEADS :]
    count = 2 * len(distances) - 1
    others, refs = refs[:count], refs[count:]
    if halo:
        halves, refs = refs[:2], refs[2:]
    total_ref, key_ref, value_ref, query_ref, grad_ref, score_ref, dprob_ref, sem = refs
    mine = pl.ds(pl.multiple_of(me * HEAD_DIM, HEAD_DIM), HEAD_DIM)
    copies = []
    for distance in range(HEADS):
        rows = pl.ds(pl.multiple_of((me ^ distance) * tok + halo, tok), tok)
        pair = (key, value)
        if distance:
            pair = [key_values[distance - 1].at[index] for index in range(2)]
        else:
            pair = (key.at[:, mine], value.at[:, mine])
        for source, target in zip(pair, (key_ref, value_ref)):
            copies.append(pltpu.make_async_copy(source, target.at[rows], sem))
    if halo:
        for side, start in ((0, 0), (1, halo + HEADS * tok)):
            for index, target in enumerate((key_ref, value_ref)):
                copies.append(
                    pltpu.make_async_copy(
                        halves[side].at[index], target.at[pl.ds(start, halo)], sem
                    )
                )
    for copy in copies:
        copy.start()
    sources = [(query.at[:, mine], grad.at[:, mine])]
    sources += [(other.at[0], other.at[1]) for other in others]
    steps = query_blocks(
        dims, place, distances, sources,
        (key_ref, value_ref, query_ref, grad_ref, score_ref, dprob_ref, total_ref, sem),
    )
    next(steps)
    total_ref[...] = jnp.zeros_like(total_ref)
    for copy in copies:
        copy.wait()
    next(steps)


def later_kernel(dims, distances, last, place, before_ref, key_ref, value_ref, *refs):
    tok, halo, _ = dims
    count = 2 * len(distances)
    others, refs = refs[:count], refs[count:]
    split = last and not halo
    if split:
        outs, refs = refs[: HEADS // 2], refs[HEADS // 2 :]
        total_ref, refs = refs[0], refs[1:]
    else:
        total_ref, refs = refs[0], refs[1:]
    sources = [(other.at[0], other.at[1]) for other in others]
    query_ref, grad_ref, score_ref, dprob_ref, sem = refs
    steps = query_blocks(
        dims, place, distances, sources,
        (key_ref, value_ref, query_ref, grad_ref, score_ref, dprob_ref, total_ref, sem),
    )
    next(steps)
    total_ref[...] = before_ref[...]
    next(steps)
    inverse_root = 1.0 / math.sqrt(HEAD_DIM)
    if split:
        pair = 2 * tok
        for distance, out in zip(slot_distances(place[0] // 2, place[2]), outs):
            start = pl.multiple_of(((place[0] // 2) ^ distance) * pair, pair)
            out[...] = (total_ref[pl.ds(start, pair)] * inverse_root).astype(jnp.bfloat16)
    elif last:
        total_ref[...] = total_ref[...] * inverse_root


def head_grads(place, arrays, key_values, query_grads, halves, groups):
    tok = arrays[0].shape[0]
    halo = HALF if halves else 0
    dims = (tok, halo, groups)
    span = HEADS * tok + 2 * halo
    window = min(span, tok + 2 * HALF)
    any_spec = pl.BlockSpec(memory_space=pltpu.HBM)
    vmem = pl.BlockSpec(memory_space=pltpu.VMEM)
    smem = pl.BlockSpec(memory_space=pltpu.SMEM)
    total = jax.ShapeDtypeStruct((span, HEAD_DIM), jnp.float32)
    low = jax.ShapeDtypeStruct((span, HEAD_DIM), jnp.bfloat16)
    piece = jax.ShapeDtypeStruct((2 * tok, HEAD_DIM), jnp.bfloat16)
    params = pltpu.CompilerParams(vmem_limit_bytes=(14 if halo else 10) * 2**20)

    def scratch(pairs):
        return [
            pltpu.VMEM((2 * pairs * tok, HEAD_DIM), jnp.bfloat16),
            pltpu.VMEM((2 * pairs * tok, HEAD_DIM), jnp.bfloat16),
            pltpu.VMEM((window, tok), jnp.float32),
            pltpu.VMEM((window, tok), jnp.float32),
        ]

    def cost(pairs):
        return pl.CostEstimate(
            flops=100 * pairs * tok * window * HEAD_DIM,
            bytes_accessed=8 * span * HEAD_DIM,
            transcendentals=2 * pairs * tok * window,
        )

    sem = [pltpu.SemaphoreType.DMA]
    state = pl.pallas_call(
        functools.partial(first_kernel, dims, (0, 1)),
        out_shape=[total, low, low],
        in_specs=[smem] + [any_spec] * (4 + HEADS - 1 + 3 + len(halves)),
        out_specs=[vmem] * 3,
        scratch_shapes=scratch(2) + sem,
        compiler_params=params,
        cost_estimate=cost(2),
        name="head_first",
    )(place, *arrays, *key_values, *query_grads[:3], *halves)
    for distance in (2, 3):
        last = distance == 3
        split = last and not halo
        others = query_grads[2 * distance - 1 : 2 * distance + 1]
        out = pl.pallas_call(
            functools.partial(later_kernel, dims, (distance,), last),
            out_shape=[piece] * (HEADS // 2) if split else [total],
            in_specs=[smem] + [vmem] * 3 + [any_spec] * 2,
            out_specs=[vmem] * (HEADS // 2 if split else 1),
            scratch_shapes=([pltpu.VMEM(total.shape, total.dtype)] if split else [])
            + scratch(1)
            + sem,
            compiler_params=params,
            cost_estimate=cost(1),
            name="head_later",
        )(place, *state, *others)
        state = [out[0], *state[1:]]
    return out if split else out[0]


def weight_kernel(place, input_ref, *refs):
    pieces, out_refs = refs[:4], refs[4:-2]
    near_ref, grad_ref = refs[-2:]
    column = place[0] // 2
    tokens = pieces[0].shape[0]
    for slot, piece in enumerate(pieces):
        document = (column % 2) ^ int(slot in (1, 2))
        side = ((column // 2) % 2) ^ int(slot < 2)
        rows = pl.ds(pl.multiple_of(document * tokens, tokens), tokens)
        grad_ref[rows, pl.ds(pl.multiple_of(side * HEAD_DIM, HEAD_DIM), HEAD_DIM)] = piece[...]
    for target in range(input_ref.shape[0]):
        product = jnp.dot(
            input_ref[target], grad_ref[...], preferred_element_type=jnp.float32
        )
        out_refs[target][...] = product.astype(out_refs[target].dtype)
        if target == 0:
            near_ref[...] = product


def weight_parts(place, inputs, pieces, dtype):
    targets, share, depth = inputs.shape
    width = 2 * HEAD_DIM
    vmem = pl.BlockSpec(memory_space=pltpu.VMEM)
    return pl.pallas_call(
        weight_kernel,
        out_shape=[jax.ShapeDtypeStruct((share, width), dtype)] * targets
        + [jax.ShapeDtypeStruct((share, width), jnp.float32)],
        in_specs=[pl.BlockSpec(memory_space=pltpu.SMEM)] + [vmem] * (1 + len(pieces)),
        out_specs=[vmem] * (targets + 1),
        scratch_shapes=[pltpu.VMEM((depth, width), jnp.bfloat16)],
        compiler_params=pltpu.CompilerParams(vmem_limit_bytes=8 * 2**20),
        cost_estimate=pl.CostEstimate(
            flops=2 * targets * share * depth * width,
            bytes_accessed=2 * depth * (width + targets * share),
            transcendentals=0,
        ),
        name="weight_parts",
    )(place, inputs, *pieces)


def sum_kernel(place, *refs):
    keep_ref, give_ref = refs[-2:]
    share = keep_ref.shape[0]
    for out_ref, core in ((give_ref, 1 - place[2]), (keep_ref, place[2])):
        rows = pl.ds(pl.multiple_of(core * share, share), share)
        total = refs[0][rows]
        for part in refs[1:-2]:
            total = total + part[rows].astype(jnp.float32)
        out_ref[...] = total


def summed(place, parts):
    share, width = parts[0].shape
    vmem = pl.BlockSpec(memory_space=pltpu.VMEM)
    return pl.pallas_call(
        sum_kernel,
        out_shape=[jax.ShapeDtypeStruct((share // 2, width), jnp.float32)] * 2,
        in_specs=[pl.BlockSpec(memory_space=pltpu.SMEM)] + [vmem] * len(parts),
        out_specs=[vmem] * 2,
        compiler_params=pltpu.CompilerParams(vmem_limit_bytes=4 * 2**20),
        name="summed",
    )(place, *parts)


def place_kernel(place, *refs):
    out_ref = refs[-1]
    for index, ref in enumerate(refs[:-1]):
        parity, core = (place[0] % 2) ^ (index // 2), place[2] ^ (index % 2)
        for column in range(HEADS // 4):
            start = pl.multiple_of((4 * column + 2 * core + parity) * HEAD_DIM, HEAD_DIM)
            out_ref[:, pl.ds(start, HEAD_DIM)] = ref[
                :, column * HEAD_DIM : (column + 1) * HEAD_DIM
            ]


def placed(place, *parts):
    share, width = parts[0].shape
    vmem = pl.BlockSpec(memory_space=pltpu.VMEM)
    return pl.pallas_call(
        place_kernel,
        out_shape=jax.ShapeDtypeStruct((share, 4 * width), jnp.float32),
        in_specs=[pl.BlockSpec(memory_space=pltpu.SMEM)] + [vmem] * len(parts),
        out_specs=vmem,
        compiler_params=pltpu.CompilerParams(vmem_limit_bytes=4 * 2**20),
        name="placed",
    )(place, *parts)


def ordered(first, own, other, axis):
    return jnp.where(first == 0, jnp.stack([own, other], axis), jnp.stack([other, own], axis))


def gathered_inputs(layer_input, me, parity, core, groups):
    tok, width = layer_input.shape
    columns = lax.axis_size("seq") // 2
    share = width // (columns * 4)
    shaped = layer_input.reshape(tok, columns, 2, 2, share)
    keep = lax.dynamic_index_in_dim(shaped, parity, 2, keepdims=False)
    give = lax.dynamic_index_in_dim(shaped, 1 - parity, 2, keepdims=False)
    both = ordered(parity, keep, exchange(give, "seq", 1), 0)
    both = both.reshape(2 * tok, columns, 2 * share)
    full = ordered(core, both, exchange(both, "dp", 1), 0)
    full = full.reshape(4 * tok, columns, 2 * share).transpose(1, 2, 0)
    if groups == 1:
        here = me // 2
        full = jnp.stack(
            [
                lax.dynamic_index_in_dim(full, here ^ distance, 0, keepdims=False)
                for distance in range(columns)
            ]
        )
    return full


def after(*values):
    return lax.optimization_barrier(values)


def local(queries, key_states, value_states, out_grad, layer_input):
    seq_count = lax.axis_size("seq")
    groups = seq_count // HEADS
    tok = queries.shape[1]
    index = lax.axis_index("seq")
    core = lax.axis_index("dp")
    me = index % HEADS
    group = index // HEADS
    parity = index % 2
    place = jnp.stack([me, group, core]).astype(jnp.int32)
    arrays = [array[0] for array in (queries, key_states, value_states, out_grad)]

    def sent(pieces, distances):
        return {d: exchange(pieces[d], "seq", d) for d in distances}

    keys, values = arrays[1:3]
    source = layer_input[0]
    width = source.shape[1]
    every = (6, 7, 4, 5, 2, 3, 1)
    direct = groups == 1 and width == HEADS * 2 * HEAD_DIM
    if direct:
        pieces = split_heads(place, keys, values, every)
        key_values = sent(pieces, (6, 7, 1, 2, 3))
        for first, second in ((6, 4), (7, 5)):
            key_values[first], pieces[second] = after(key_values[first], pieces[second])
        key_values |= sent(pieces, (4, 5))
        key_values[1], source = after(key_values[1], source)
        block = jax.ShapeDtypeStruct((HEADS, tok, HEAD_DIM), source.dtype)
        keep, give = moved(sides_kernel, [block] * 2, place, source)
        received = exchange(give, "seq", 1)
        sides = [keep, exchange(keep, "dp", 1), received, exchange(received, "dp", 1)]
        shape = (HEADS // 2, 2 * HEAD_DIM, 4 * tok)
        turned = jax.ShapeDtypeStruct(shape, source.dtype)
    else:
        key_values = sent(split_heads(place, keys, values, every), every)
        inputs = gathered_inputs(source, me, parity, core, groups)
    pieces = split_heads(place, arrays[0], arrays[3], every)
    for first, second in ((1, 1), (2, 2), (3, 3), (4, 4), (5, 5), (5, 6), (5, 7)):
        key_values[first], pieces[second] = after(key_values[first], pieces[second])
    if direct:
        sides[1], pieces[7] = after(sides[1], pieces[7])
    query_grads = sent(pieces, every)
    if direct:
        inputs = moved(turned_kernel, [turned], place, *sides)[0]
        query_grads[7], inputs = after(query_grads[7], inputs)
    key_values = [key_values[d] for d in range(1, HEADS)]
    query_grads = [query_grads[d] for d in range(1, HEADS)]
    halves = []
    if groups > 1:
        mine = [lax.dynamic_slice_in_dim(a, me * HEAD_DIM, HEAD_DIM, 1) for a in arrays[1:3]]
        by_distance = jnp.stack([jnp.stack(mine), *key_values])
        rows = jnp.stack(
            [
                lax.dynamic_index_in_dim(by_distance, me ^ block, 0, keepdims=False)
                for block in range(HEADS)
            ]
        )
        rows = rows.transpose(1, 0, 2, 3).reshape(2, HEADS * tok, HEAD_DIM)
        ahead = [(source, source + HEADS) for source in range(seq_count - HEADS)]
        back = [(source + HEADS, source) for source in range(seq_count - HEADS)]
        halves = [
            lax.ppermute(rows[:, -HALF:], "seq", ahead),
            lax.ppermute(rows[:, :HALF], "seq", back),
        ]
    grads = head_grads(place, arrays, key_values, query_grads, halves, groups)
    if groups > 1:
        from_after = lax.ppermute(grads[:HALF].astype(jnp.bfloat16), "seq", back)
        from_before = lax.ppermute(grads[-HALF:].astype(jnp.bfloat16), "seq", ahead)
        inner = grads[HALF:-HALF]
        inner = inner.at[-HALF:].add(from_after.astype(jnp.float32))
        inner = inner.at[:HALF].add(from_before.astype(jnp.float32))
        inner = inner.astype(jnp.bfloat16)
        grads = [
            lax.dynamic_slice_in_dim(inner, ((me // 2) ^ distance) * 2 * tok, 2 * tok, 0)
            for distance in slot_distances(me // 2, core)
        ]

    near = [
        lax.ppermute(piece, ("seq", "dp"), slot_route(slot)) for slot, piece in enumerate(grads)
    ]
    far = [exchange(piece, "seq", 1) for piece in near[2:]]
    held = after(near[0], near[1], *near[2:], *far)
    far = list(held[4:])
    far = [exchange(piece, "seq", 1) for piece in held[:2]] + far

    if groups > 1:
        members = [list(range(first, seq_count, 2)) for first in (0, 1)]

        def scattered(pieces):
            parts = weight_parts(place, inputs, pieces, jnp.float32)[:-1]
            rows = lax.psum_scatter(
                jnp.concatenate(parts), "seq", scatter_dimension=0,
                axis_index_groups=members, tiled=True,
            )
            rows = rows.reshape(2, -1, HEADS // 4, HEAD_DIM)
            keep = lax.dynamic_index_in_dim(rows, core, 0, keepdims=False)
            give = lax.dynamic_index_in_dim(rows, 1 - core, 0, keepdims=False)
            return ordered(core, keep, exchange(give, "dp", 1), 2)

        result = ordered(parity, scattered(near), scattered(far), 3)
        return result.reshape(result.shape[0], HEADS * HEAD_DIM)

    def spread(pieces):
        *parts, total = weight_parts(place, inputs, pieces, jnp.bfloat16)
        return [total] + [
            exchange(parts[distance], "seq", 2 * distance) for distance in (3, 2, 1)
        ]

    first = spread(near)
    far, first[1] = after(far, first[1])
    second = spread(far)
    near_keep, near_give = summed(place, first)
    far_keep, far_give = summed(place, second)
    near_other, far_other = exchange(near_give, "dp", 1), exchange(far_give, "dp", 1)
    return placed(place, near_keep, near_other, far_keep, far_other)


def solution(mesh):
    spec = P(("parts", "dp"), "seq", None)
    out_specs = P(("parts", "seq", "dp"), None)
    return jax.shard_map(
        local, mesh=mesh, in_specs=(spec,) * 5, out_specs=out_specs, check_vma=False
    )
```

```python
import functools
import math

import jax
import jax.numpy as jnp
from jax import lax
from jax.experimental import pallas as pl
from jax.experimental.pallas import tpu as pltpu
from jax.sharding import PartitionSpec as P

HEADS = 8
HEAD_DIM = 128
HALF = 1024
NEG = -1e30
CHUNK = 2
SKIP = 2
NT = (((1,), (1,)), ((), ()))


def exchange(value, axis, distance):
    count = lax.axis_size(axis)
    return lax.ppermute(value, axis, [(source, source ^ distance) for source in range(count)])


def fold_rows(value, op):
    rows = value.shape[0]
    total = value[0:8]
    for start in range(8, rows, 8):
        total = op(total, value[start : start + 8])
    return total


def slot_distances(column, core):
    aside = (column % 2) ^ core
    return (2 + aside, 3 - aside, 1 - aside, aside)


def slot_route(slot):
    pairs = []
    for source in range(lax.axis_size("seq")):
        for core in range(2):
            column, parity = source // 2, source % 2
            target = column ^ slot_distances(column, core)[slot]
            pairs.append((2 * source + core, 2 * (2 * target + parity) + column % 2))
    return pairs


def columns(array, block):
    return array[:, pl.ds(pl.multiple_of(block * HEAD_DIM, HEAD_DIM), HEAD_DIM)]


def split_kernel(distances, place, left, right, *refs):
    outs, sem = refs[:-1], refs[-1]
    copies = []
    for distance, out in zip(distances, outs):
        start = pl.multiple_of((place[0] ^ distance) * HEAD_DIM, HEAD_DIM)
        for index, array in enumerate((left, right)):
            piece = array.at[:, pl.ds(start, HEAD_DIM)]
            copies.append(pltpu.make_async_copy(piece, out.at[index], sem))
    for copy in copies:
        copy.start()
    for copy in copies:
        copy.wait()


def split_heads(place, left, right, distances):
    vmem = pl.BlockSpec(memory_space=pltpu.VMEM)
    hbm = pl.BlockSpec(memory_space=pltpu.HBM)
    tok = left.shape[0]
    shape = jax.ShapeDtypeStruct((2, tok, HEAD_DIM), left.dtype)
    pieces = pl.pallas_call(
        functools.partial(split_kernel, distances),
        out_shape=[shape] * len(distances),
        in_specs=[pl.BlockSpec(memory_space=pltpu.SMEM), hbm, hbm],
        out_specs=[vmem] * len(distances),
        scratch_shapes=[pltpu.SemaphoreType.DMA],
        compiler_params=pltpu.CompilerParams(vmem_limit_bytes=4 * 2**20),
        name="split_heads",
    )(place, left, right)
    return dict(zip(distances, pieces))


def sides_kernel(place, inputs, keep, give):
    for column in range(HEADS // 2):
        for core in range(2):
            device = 2 * column + place[0] % 2
            keep[2 * column + core] = columns(inputs, 2 * device + core)
            device = 2 * column + 1 - place[0] % 2
            give[2 * column + core] = columns(inputs, 2 * device + core)


def turned_kernel(place, keep, keep_other, received, received_other, out):
    tok = keep.shape[1]
    parity, core = place[0] % 2, place[2]
    for distance in range(HEADS // 2):
        for target in range(2):
            index = 2 * ((place[0] // 2) ^ distance) + target
            rows = slice(target * HEAD_DIM, (target + 1) * HEAD_DIM)
            for document, side, blocks in (
                (core, parity, keep),
                (1 - core, parity, keep_other),
                (core, 1 - parity, received),
                (1 - core, 1 - parity, received_other),
            ):
                start = pl.multiple_of((2 * document + side) * tok, tok)
                out[distance, rows, pl.ds(start, tok)] = blocks[index].T


def moved(kernel, shapes, *operands):
    vmem = pl.BlockSpec(memory_space=pltpu.VMEM)
    return pl.pallas_call(
        kernel,
        out_shape=shapes,
        in_specs=[pl.BlockSpec(memory_space=pltpu.SMEM)] + [vmem] * (len(operands) - 1),
        out_specs=[vmem] * len(shapes),
        compiler_params=pltpu.CompilerParams(vmem_limit_bytes=6 * 2**20),
        name="moved",
    )(*operands)


def head_block(dims, place, b, edge, query, grad, key_ref, value_ref, score_ref, dprob_ref, total_ref):
    tok, halo, groups = dims
    shift = halo // tok
    reach = HALF // tok
    scale = math.log2(math.e) / math.sqrt(HEAD_DIM)
    ahead = lax.broadcasted_iota(jnp.int32, (tok, tok), 0)
    ahead = ahead - lax.broadcasted_iota(jnp.int32, (tok, tok), 1)
    if halo:
        first, count, below, above = b + shift - reach, 2 * reach + 1, 1, 2 * reach
    elif edge:
        first, count = jnp.where(b >= reach, SKIP, 0), HEADS - SKIP
        below, above = HEADS - reach - SKIP, reach
    else:
        first, count, below, above = 0, HEADS, SKIP, HEADS - SKIP
    chunks = [range(start, min(start + CHUNK, count)) for start in range(0, count, CHUNK)]

    def rows_of(chunk):
        start = (first + chunk[0]) * tok
        traced = halo or edge
        return pl.ds(pl.multiple_of(start, tok) if traced else start, len(chunk) * tok)

    def held(at):
        return slice(at * tok, (at + 1) * tok)

    top = None
    for chunk in chunks:
        scores = lax.dot_general(
            key_ref[rows_of(chunk)], query, NT, preferred_element_type=jnp.float32
        )
        for at in chunk:
            score = scores[held(at - chunk[0])]
            distance = first + at - shift - b
            if at < below:
                score = jnp.where(ahead >= -HALF - distance * tok, score, NEG)
            if at >= above:
                score = jnp.where(ahead <= HALF - distance * tok, score, NEG)
            if halo:
                inside = (first + at >= shift) | (place[1] > 0)
                inside &= (first + at < shift + HEADS) | (place[1] < groups - 1)
                score = jnp.where(inside, score, NEG)
            score_ref[held(at)] = score
            part = fold_rows(score, jnp.maximum)
            top = part if top is None else jnp.maximum(top, part)
    top = jnp.max(top, axis=0, keepdims=True) * scale
    weight_sum = jnp.zeros((8, tok), jnp.float32)
    delta_sum = jnp.zeros((8, tok), jnp.float32)
    for chunk in chunks:
        dprobs = lax.dot_general(
            value_ref[rows_of(chunk)], grad, NT, preferred_element_type=jnp.float32
        )
        for at in chunk:
            dprob = dprobs[held(at - chunk[0])]
            weight = jnp.exp2(score_ref[held(at)] * scale - top)
            score_ref[held(at)] = weight
            dprob_ref[held(at)] = dprob
            weight_sum = weight_sum + fold_rows(weight, jnp.add)
            delta_sum = delta_sum + fold_rows(weight * dprob, jnp.add)
    inverse = 1.0 / jnp.sum(weight_sum, axis=0, keepdims=True)
    delta = jnp.sum(delta_sum, axis=0, keepdims=True) * inverse
    for chunk in chunks:
        held_rows = slice(chunk[0] * tok, (chunk[-1] + 1) * tok)
        prob = score_ref[held_rows] * inverse
        dscore = prob * (dprob_ref[held_rows] - delta)
        total_ref[rows_of(chunk)] += jnp.dot(
            dscore.astype(jnp.bfloat16), query, preferred_element_type=jnp.float32
        )


def query_blocks(dims, place, distances, sources, refs):
    tok = dims[0]
    me = place[0]
    key_ref, value_ref, query_ref, grad_ref, score_ref, dprob_ref, total_ref, sem = refs
    copies = []
    for slot, source in enumerate(sources):
        rows = slice(slot * tok, (slot + 1) * tok)
        for target, piece in zip((query_ref, grad_ref), source):
            copies.append(pltpu.make_async_copy(piece, target.at[rows], sem))
    for copy in copies:
        copy.start()
    yield
    for copy in copies:
        copy.wait()

    def block(slot, distance):
        rows = pl.ds(pl.multiple_of(slot * tok, tok), tok)
        index = me ^ distance

        def work(edge):
            head_block(
                dims, place, index, edge, query_ref[rows], grad_ref[rows], key_ref, value_ref,
                score_ref, dprob_ref, total_ref,
            )

        if dims[1]:
            work(False)
            return
        reach = HALF // tok
        edge = (index < HEADS - SKIP - reach) | (index >= reach + SKIP)
        pl.when(edge)(lambda: work(True))
        pl.when(jnp.logical_not(edge))(lambda: work(False))

    @pl.loop(0, 2 * len(distances))
    def _(slot):
        block(slot, 2 * distances[0] + slot)

    yield


def first_kernel(dims, distances, place, *refs):
    tok, halo, _ = dims
    me = place[0]
    query, key, value, grad = refs[:4]
    key_values, refs = refs[4 : 3 + HEADS], refs[3 + HEADS :]
    count = 2 * len(distances) - 1
    others, refs = refs[:count], refs[count:]
    if halo:
        halves, refs = refs[:2], refs[2:]
    total_ref, key_ref, value_ref, query_ref, grad_ref, score_ref, dprob_ref, sem = refs
    mine = pl.ds(pl.multiple_of(me * HEAD_DIM, HEAD_DIM), HEAD_DIM)
    copies = []
    for distance in range(HEADS):
        rows = pl.ds(pl.multiple_of((me ^ distance) * tok + halo, tok), tok)
        pair = (key, value)
        if distance:
            pair = [key_values[distance - 1].at[index] for index in range(2)]
        else:
            pair = (key.at[:, mine], value.at[:, mine])
        for source, target in zip(pair, (key_ref, value_ref)):
            copies.append(pltpu.make_async_copy(source, target.at[rows], sem))
    if halo:
        for side, start in ((0, 0), (1, halo + HEADS * tok)):
            for index, target in enumerate((key_ref, value_ref)):
                copies.append(
                    pltpu.make_async_copy(
                        halves[side].at[index], target.at[pl.ds(start, halo)], sem
                    )
                )
    for copy in copies:
        copy.start()
    sources = [(query.at[:, mine], grad.at[:, mine])]
    sources += [(other.at[0], other.at[1]) for other in others]
    steps = query_blocks(
        dims, place, distances, sources,
        (key_ref, value_ref, query_ref, grad_ref, score_ref, dprob_ref, total_ref, sem),
    )
    next(steps)
    total_ref[...] = jnp.zeros_like(total_ref)
    for copy in copies:
        copy.wait()
    next(steps)


def later_kernel(dims, distances, last, place, before_ref, key_ref, value_ref, *refs):
    tok, halo, _ = dims
    count = 2 * len(distances)
    others, refs = refs[:count], refs[count:]
    split = last and not halo
    if split:
        outs, refs = refs[: HEADS // 2], refs[HEADS // 2 :]
        total_ref, refs = refs[0], refs[1:]
    else:
        total_ref, refs = refs[0], refs[1:]
    sources = [(other.at[0], other.at[1]) for other in others]
    query_ref, grad_ref, score_ref, dprob_ref, sem = refs
    steps = query_blocks(
        dims, place, distances, sources,
        (key_ref, value_ref, query_ref, grad_ref, score_ref, dprob_ref, total_ref, sem),
    )
    next(steps)
    total_ref[...] = before_ref[...]
    next(steps)
    inverse_root = 1.0 / math.sqrt(HEAD_DIM)
    if split:
        pair = 2 * tok
        for distance, out in zip(slot_distances(place[0] // 2, place[2]), outs):
            start = pl.multiple_of(((place[0] // 2) ^ distance) * pair, pair)
            out[...] = (total_ref[pl.ds(start, pair)] * inverse_root).astype(jnp.bfloat16)
    elif last:
        total_ref[...] = total_ref[...] * inverse_root


def head_grads(place, arrays, key_values, query_grads, halves, groups):
    tok = arrays[0].shape[0]
    halo = HALF if halves else 0
    dims = (tok, halo, groups)
    span = HEADS * tok + 2 * halo
    window = min(span, tok + 2 * HALF)
    any_spec = pl.BlockSpec(memory_space=pltpu.HBM)
    vmem = pl.BlockSpec(memory_space=pltpu.VMEM)
    smem = pl.BlockSpec(memory_space=pltpu.SMEM)
    total = jax.ShapeDtypeStruct((span, HEAD_DIM), jnp.float32)
    low = jax.ShapeDtypeStruct((span, HEAD_DIM), jnp.bfloat16)
    piece = jax.ShapeDtypeStruct((2 * tok, HEAD_DIM), jnp.bfloat16)
    params = pltpu.CompilerParams(vmem_limit_bytes=(14 if halo else 10) * 2**20)

    def scratch(pairs):
        return [
            pltpu.VMEM((2 * pairs * tok, HEAD_DIM), jnp.bfloat16),
            pltpu.VMEM((2 * pairs * tok, HEAD_DIM), jnp.bfloat16),
            pltpu.VMEM((window, tok), jnp.float32),
            pltpu.VMEM((window, tok), jnp.float32),
        ]

    def cost(pairs):
        return pl.CostEstimate(
            flops=100 * pairs * tok * window * HEAD_DIM,
            bytes_accessed=8 * span * HEAD_DIM,
            transcendentals=2 * pairs * tok * window,
        )

    sem = [pltpu.SemaphoreType.DMA]
    state = pl.pallas_call(
        functools.partial(first_kernel, dims, (0, 1)),
        out_shape=[total, low, low],
        in_specs=[smem] + [any_spec] * (4 + HEADS - 1 + 3 + len(halves)),
        out_specs=[vmem] * 3,
        scratch_shapes=scratch(2) + sem,
        compiler_params=params,
        cost_estimate=cost(2),
        name="head_first",
    )(place, *arrays, *key_values, *query_grads[:3], *halves)
    for distance in (2, 3):
        last = distance == 3
        split = last and not halo
        others = query_grads[2 * distance - 1 : 2 * distance + 1]
        out = pl.pallas_call(
            functools.partial(later_kernel, dims, (distance,), last),
            out_shape=[piece] * (HEADS // 2) if split else [total],
            in_specs=[smem] + [vmem] * 3 + [any_spec] * 2,
            out_specs=[vmem] * (HEADS // 2 if split else 1),
            scratch_shapes=([pltpu.VMEM(total.shape, total.dtype)] if split else [])
            + scratch(1)
            + sem,
            compiler_params=params,
            cost_estimate=cost(1),
            name="head_later",
        )(place, *state, *others)
        state = [out[0], *state[1:]]
    return out if split else out[0]


def weight_kernel(targets, place, input_ref, *refs):
    pieces, out_refs, grad_ref = refs[:4], refs[4:-1], refs[-1]
    column = place[0] // 2
    tokens = pieces[0].shape[0]
    for slot, piece in enumerate(pieces):
        document = (column % 2) ^ int(slot in (1, 2))
        side = ((column // 2) % 2) ^ int(slot < 2)
        rows = pl.ds(pl.multiple_of(document * tokens, tokens), tokens)
        grad_ref[rows, pl.ds(pl.multiple_of(side * HEAD_DIM, HEAD_DIM), HEAD_DIM)] = piece[...]
    for target, out_ref in zip(targets, out_refs):
        product = jnp.dot(
            input_ref[target], grad_ref[...], preferred_element_type=jnp.float32
        )
        out_ref[...] = product.astype(out_ref.dtype)


def weight_parts(place, inputs, pieces, targets, dtypes):
    _, share, depth = inputs.shape
    width = 2 * HEAD_DIM
    vmem = pl.BlockSpec(memory_space=pltpu.VMEM)
    return pl.pallas_call(
        functools.partial(weight_kernel, targets),
        out_shape=[jax.ShapeDtypeStruct((share, width), dtype) for dtype in dtypes],
        in_specs=[pl.BlockSpec(memory_space=pltpu.SMEM)] + [vmem] * (1 + len(pieces)),
        out_specs=[vmem] * len(targets),
        scratch_shapes=[pltpu.VMEM((depth, width), jnp.bfloat16)],
        compiler_params=pltpu.CompilerParams(vmem_limit_bytes=8 * 2**20),
        cost_estimate=pl.CostEstimate(
            flops=2 * len(targets) * share * depth * width,
            bytes_accessed=2 * depth * (width + len(targets) * share),
            transcendentals=0,
        ),
        name="weight_parts",
    )(place, inputs, *pieces)


def sum_kernel(place, *refs):
    keep_ref, give_ref = refs[-2:]
    share = keep_ref.shape[0]
    for out_ref, core in ((give_ref, 1 - place[2]), (keep_ref, place[2])):
        rows = pl.ds(pl.multiple_of(core * share, share), share)
        total = refs[0][rows]
        for part in refs[1:-2]:
            total = total + part[rows].astype(jnp.float32)
        out_ref[...] = total


def summed(place, parts):
    share, width = parts[0].shape
    vmem = pl.BlockSpec(memory_space=pltpu.VMEM)
    return pl.pallas_call(
        sum_kernel,
        out_shape=[jax.ShapeDtypeStruct((share // 2, width), jnp.float32)] * 2,
        in_specs=[pl.BlockSpec(memory_space=pltpu.SMEM)] + [vmem] * len(parts),
        out_specs=[vmem] * 2,
        compiler_params=pltpu.CompilerParams(vmem_limit_bytes=4 * 2**20),
        name="summed",
    )(place, *parts)


def place_kernel(side, place, *refs):
    parts, out_ref, sem = refs[:2], refs[-2], refs[-1]
    parity = (place[0] % 2) ^ side
    copies = []
    for index, ref in enumerate(parts):
        for column in range(HEADS // 4):
            block = 4 * column + 2 * (place[2] ^ index) + parity
            start = pl.multiple_of(block * HEAD_DIM, HEAD_DIM)
            source = ref.at[:, column * HEAD_DIM : (column + 1) * HEAD_DIM]
            target = out_ref.at[:, pl.ds(start, HEAD_DIM)]
            copies.append(pltpu.make_async_copy(source, target, sem))
    for copy in copies:
        copy.start()
    for copy in copies:
        copy.wait()


def placed(place, side, keep, other, before=None):
    share, width = keep.shape
    vmem = pl.BlockSpec(memory_space=pltpu.VMEM)
    hbm = pl.BlockSpec(memory_space=pltpu.HBM)
    rest = [] if before is None else [before]
    return pl.pallas_call(
        functools.partial(place_kernel, side),
        out_shape=jax.ShapeDtypeStruct((share, 4 * width), jnp.float32),
        in_specs=[pl.BlockSpec(memory_space=pltpu.SMEM), vmem, vmem] + [hbm] * len(rest),
        out_specs=hbm,
        scratch_shapes=[pltpu.SemaphoreType.DMA],
        input_output_aliases={3: 0} if rest else {},
        compiler_params=pltpu.CompilerParams(vmem_limit_bytes=2 * 2**20),
        name="placed",
    )(place, keep, other, *rest)


def ordered(first, own, other, axis):
    return jnp.where(first == 0, jnp.stack([own, other], axis), jnp.stack([other, own], axis))


def gathered_inputs(layer_input, me, parity, core, groups):
    tok, width = layer_input.shape
    columns = lax.axis_size("seq") // 2
    share = width // (columns * 4)
    shaped = layer_input.reshape(tok, columns, 2, 2, share)
    keep = lax.dynamic_index_in_dim(shaped, parity, 2, keepdims=False)
    give = lax.dynamic_index_in_dim(shaped, 1 - parity, 2, keepdims=False)
    both = ordered(parity, keep, exchange(give, "seq", 1), 0)
    both = both.reshape(2 * tok, columns, 2 * share)
    full = ordered(core, both, exchange(both, "dp", 1), 0)
    full = full.reshape(4 * tok, columns, 2 * share).transpose(1, 2, 0)
    if groups == 1:
        here = me // 2
        full = jnp.stack(
            [
                lax.dynamic_index_in_dim(full, here ^ distance, 0, keepdims=False)
                for distance in range(columns)
            ]
        )
    return full


def after(*values):
    return lax.optimization_barrier(values)


def local(queries, key_states, value_states, out_grad, layer_input):
    seq_count = lax.axis_size("seq")
    groups = seq_count // HEADS
    tok = queries.shape[1]
    index = lax.axis_index("seq")
    core = lax.axis_index("dp")
    me = index % HEADS
    group = index // HEADS
    parity = index % 2
    place = jnp.stack([me, group, core]).astype(jnp.int32)
    arrays = [array[0] for array in (queries, key_states, value_states, out_grad)]

    def sent(pieces, distances):
        return {d: exchange(pieces[d], "seq", d) for d in distances}

    keys, values = arrays[1:3]
    source = layer_input[0]
    width = source.shape[1]
    every = (6, 7, 4, 5, 2, 3, 1)
    direct = groups == 1 and width == HEADS * 2 * HEAD_DIM
    if direct:
        pieces = split_heads(place, keys, values, every)
        key_values = sent(pieces, (6, 7, 1, 2, 3))
        for first, second in ((6, 4), (7, 5)):
            key_values[first], pieces[second] = after(key_values[first], pieces[second])
        key_values |= sent(pieces, (4, 5))
        key_values[1], source = after(key_values[1], source)
        block = jax.ShapeDtypeStruct((HEADS, tok, HEAD_DIM), source.dtype)
        keep, give = moved(sides_kernel, [block] * 2, place, source)
        received = exchange(give, "seq", 1)
        sides = [keep, exchange(keep, "dp", 1), received, exchange(received, "dp", 1)]
        shape = (HEADS // 2, 2 * HEAD_DIM, 4 * tok)
        turned = jax.ShapeDtypeStruct(shape, source.dtype)
    else:
        key_values = sent(split_heads(place, keys, values, every), every)
        inputs = gathered_inputs(source, me, parity, core, groups)
    pieces = split_heads(place, arrays[0], arrays[3], every)
    for first, second in ((1, 1), (2, 2), (3, 3), (4, 4), (5, 5), (5, 6), (5, 7)):
        key_values[first], pieces[second] = after(key_values[first], pieces[second])
    if direct:
        sides[1], pieces[7] = after(sides[1], pieces[7])
    query_grads = sent(pieces, every)
    if direct:
        inputs = moved(turned_kernel, [turned], place, *sides)[0]
        query_grads[7], inputs = after(query_grads[7], inputs)
    key_values = [key_values[d] for d in range(1, HEADS)]
    query_grads = [query_grads[d] for d in range(1, HEADS)]
    halves = []
    if groups > 1:
        mine = [lax.dynamic_slice_in_dim(a, me * HEAD_DIM, HEAD_DIM, 1) for a in arrays[1:3]]
        by_distance = jnp.stack([jnp.stack(mine), *key_values])
        rows = jnp.stack(
            [
                lax.dynamic_index_in_dim(by_distance, me ^ block, 0, keepdims=False)
                for block in range(HEADS)
            ]
        )
        rows = rows.transpose(1, 0, 2, 3).reshape(2, HEADS * tok, HEAD_DIM)
        ahead = [(source, source + HEADS) for source in range(seq_count - HEADS)]
        back = [(source + HEADS, source) for source in range(seq_count - HEADS)]
        halves = [
            lax.ppermute(rows[:, -HALF:], "seq", ahead),
            lax.ppermute(rows[:, :HALF], "seq", back),
        ]
    grads = head_grads(place, arrays, key_values, query_grads, halves, groups)
    if groups > 1:
        from_after = lax.ppermute(grads[:HALF].astype(jnp.bfloat16), "seq", back)
        from_before = lax.ppermute(grads[-HALF:].astype(jnp.bfloat16), "seq", ahead)
        inner = grads[HALF:-HALF]
        inner = inner.at[-HALF:].add(from_after.astype(jnp.float32))
        inner = inner.at[:HALF].add(from_before.astype(jnp.float32))
        inner = inner.astype(jnp.bfloat16)
        grads = [
            lax.dynamic_slice_in_dim(inner, ((me // 2) ^ distance) * 2 * tok, 2 * tok, 0)
            for distance in slot_distances(me // 2, core)
        ]

    near = [
        lax.ppermute(piece, ("seq", "dp"), slot_route(slot)) for slot, piece in enumerate(grads)
    ]
    far = [exchange(piece, "seq", 1) for piece in near[2:]]
    held = after(near[0], near[1], *near[2:], *far)
    far = list(held[4:])
    far = [exchange(piece, "seq", 1) for piece in held[:2]] + far

    if groups > 1:
        members = [list(range(first, seq_count, 2)) for first in (0, 1)]

        def scattered(pieces):
            targets = range(inputs.shape[0])
            parts = weight_parts(place, inputs, pieces, targets, [jnp.float32] * len(targets))
            rows = lax.psum_scatter(
                jnp.concatenate(parts), "seq", scatter_dimension=0,
                axis_index_groups=members, tiled=True,
            )
            rows = rows.reshape(2, -1, HEADS // 4, HEAD_DIM)
            keep = lax.dynamic_index_in_dim(rows, core, 0, keepdims=False)
            give = lax.dynamic_index_in_dim(rows, 1 - core, 0, keepdims=False)
            return ordered(core, keep, exchange(give, "dp", 1), 2)

        result = ordered(parity, scattered(near), scattered(far), 3)
        return result.reshape(result.shape[0], HEADS * HEAD_DIM)

    def spread(pieces):
        low = jnp.bfloat16
        across = weight_parts(place, inputs, pieces, (3, 2), (low, low))
        beside, total = weight_parts(place, inputs, pieces, (1, 0), (low, jnp.float32))
        parts = zip((3, 2, 1), (*across, beside))
        return [total] + [exchange(part, "seq", 2 * distance) for distance, part in parts]

    first = spread(near)
    far, first[1] = after(far, first[1])
    second = spread(far)
    near_keep, near_give = summed(place, first)
    far_keep, far_give = summed(place, second)
    half = placed(place, 0, near_keep, exchange(near_give, "dp", 1))
    return placed(place, 1, far_keep, exchange(far_give, "dp", 1), half)


def solution(mesh):
    spec = P(("parts", "dp"), "seq", None)
    out_specs = P(("parts", "seq", "dp"), None)
    return jax.shard_map(
        local, mesh=mesh, in_specs=(spec,) * 5, out_specs=out_specs, check_vma=False
    )
```

```python
import functools
import math

import jax
import jax.numpy as jnp
from jax import lax
from jax.experimental import pallas as pl
from jax.experimental.pallas import tpu as pltpu
from jax.sharding import PartitionSpec as P

HEADS = 8
HEAD_DIM = 128
HALF = 1024
NEG = -1e30
CHUNK = 2
SKIP = 2
NT = (((1,), (1,)), ((), ()))


def exchange(value, axis, distance):
    count = lax.axis_size(axis)
    return lax.ppermute(value, axis, [(source, source ^ distance) for source in range(count)])


def fold_rows(value, op):
    rows = value.shape[0]
    total = value[0:8]
    for start in range(8, rows, 8):
        total = op(total, value[start : start + 8])
    return total


def slot_distances(column, core):
    aside = (column % 2) ^ core
    return (2 + aside, 3 - aside, 1 - aside, aside)


def slot_route(slot):
    pairs = []
    for source in range(lax.axis_size("seq")):
        for core in range(2):
            column, parity = source // 2, source % 2
            target = column ^ slot_distances(column, core)[slot]
            pairs.append((2 * source + core, 2 * (2 * target + parity) + column % 2))
    return pairs


def columns(array, block):
    return array[:, pl.ds(pl.multiple_of(block * HEAD_DIM, HEAD_DIM), HEAD_DIM)]


def split_kernel(distances, place, left, right, *refs):
    outs, sem = refs[:-1], refs[-1]
    copies = []
    for distance, out in zip(distances, outs):
        start = pl.multiple_of((place[0] ^ distance) * HEAD_DIM, HEAD_DIM)
        for index, array in enumerate((left, right)):
            piece = array.at[:, pl.ds(start, HEAD_DIM)]
            copies.append(pltpu.make_async_copy(piece, out.at[index], sem))
    for copy in copies:
        copy.start()
    for copy in copies:
        copy.wait()


def split_heads(place, left, right, distances):
    vmem = pl.BlockSpec(memory_space=pltpu.VMEM)
    hbm = pl.BlockSpec(memory_space=pltpu.HBM)
    tok = left.shape[0]
    shape = jax.ShapeDtypeStruct((2, tok, HEAD_DIM), left.dtype)
    pieces = pl.pallas_call(
        functools.partial(split_kernel, distances),
        out_shape=[shape] * len(distances),
        in_specs=[pl.BlockSpec(memory_space=pltpu.SMEM), hbm, hbm],
        out_specs=[vmem] * len(distances),
        scratch_shapes=[pltpu.SemaphoreType.DMA],
        compiler_params=pltpu.CompilerParams(vmem_limit_bytes=4 * 2**20),
        name="split_heads",
    )(place, left, right)
    return dict(zip(distances, pieces))


def sides_kernel(place, inputs, keep, give):
    for column in range(HEADS // 2):
        for core in range(2):
            device = 2 * column + place[0] % 2
            keep[2 * column + core] = columns(inputs, 2 * device + core)
            device = 2 * column + 1 - place[0] % 2
            give[2 * column + core] = columns(inputs, 2 * device + core)


def turned_kernel(place, keep, keep_other, received, received_other, out):
    tok = keep.shape[1]
    parity, core = place[0] % 2, place[2]
    for distance in range(HEADS // 2):
        for target in range(2):
            index = 2 * ((place[0] // 2) ^ distance) + target
            rows = slice(target * HEAD_DIM, (target + 1) * HEAD_DIM)
            for document, side, blocks in (
                (core, parity, keep),
                (1 - core, parity, keep_other),
                (core, 1 - parity, received),
                (1 - core, 1 - parity, received_other),
            ):
                start = pl.multiple_of((2 * document + side) * tok, tok)
                out[distance, rows, pl.ds(start, tok)] = blocks[index].T


def moved(kernel, shapes, *operands):
    vmem = pl.BlockSpec(memory_space=pltpu.VMEM)
    return pl.pallas_call(
        kernel,
        out_shape=shapes,
        in_specs=[pl.BlockSpec(memory_space=pltpu.SMEM)] + [vmem] * (len(operands) - 1),
        out_specs=[vmem] * len(shapes),
        compiler_params=pltpu.CompilerParams(vmem_limit_bytes=6 * 2**20),
        name="moved",
    )(*operands)


def head_block(dims, place, b, edge, query, grad, key_ref, value_ref, score_ref, dprob_ref, total_ref):
    tok, halo, groups = dims
    shift = halo // tok
    reach = HALF // tok
    scale = math.log2(math.e) / math.sqrt(HEAD_DIM)
    ahead = lax.broadcasted_iota(jnp.int32, (tok, tok), 0)
    ahead = ahead - lax.broadcasted_iota(jnp.int32, (tok, tok), 1)
    if halo:
        first, count, below, above = b + shift - reach, 2 * reach + 1, 1, 2 * reach
    elif edge:
        first, count = jnp.where(b >= reach, SKIP, 0), HEADS - SKIP
        below, above = HEADS - reach - SKIP, reach
    else:
        first, count, below, above = 0, HEADS, SKIP, HEADS - SKIP
    chunks = [range(start, min(start + CHUNK, count)) for start in range(0, count, CHUNK)]

    def rows_of(chunk):
        start = (first + chunk[0]) * tok
        traced = halo or edge
        return pl.ds(pl.multiple_of(start, tok) if traced else start, len(chunk) * tok)

    def held(at):
        return slice(at * tok, (at + 1) * tok)

    top = None
    for chunk in chunks:
        scores = lax.dot_general(
            key_ref[rows_of(chunk)], query, NT, preferred_element_type=jnp.float32
        )
        for at in chunk:
            score = scores[held(at - chunk[0])]
            distance = first + at - shift - b
            if at < below:
                score = jnp.where(ahead >= -HALF - distance * tok, score, NEG)
            if at >= above:
                score = jnp.where(ahead <= HALF - distance * tok, score, NEG)
            if halo:
                inside = (first + at >= shift) | (place[1] > 0)
                inside &= (first + at < shift + HEADS) | (place[1] < groups - 1)
                score = jnp.where(inside, score, NEG)
            score_ref[held(at)] = score
            part = fold_rows(score, jnp.maximum)
            top = part if top is None else jnp.maximum(top, part)
    top = jnp.max(top, axis=0, keepdims=True) * scale
    weight_sum = jnp.zeros((8, tok), jnp.float32)
    delta_sum = jnp.zeros((8, tok), jnp.float32)
    for chunk in chunks:
        dprobs = lax.dot_general(
            value_ref[rows_of(chunk)], grad, NT, preferred_element_type=jnp.float32
        )
        for at in chunk:
            dprob = dprobs[held(at - chunk[0])]
            weight = jnp.exp2(score_ref[held(at)] * scale - top)
            score_ref[held(at)] = weight
            dprob_ref[held(at)] = dprob
            weight_sum = weight_sum + fold_rows(weight, jnp.add)
            delta_sum = delta_sum + fold_rows(weight * dprob, jnp.add)
    inverse = 1.0 / jnp.sum(weight_sum, axis=0, keepdims=True)
    delta = jnp.sum(delta_sum, axis=0, keepdims=True) * inverse
    for chunk in chunks:
        held_rows = slice(chunk[0] * tok, (chunk[-1] + 1) * tok)
        prob = score_ref[held_rows] * inverse
        dscore = prob * (dprob_ref[held_rows] - delta)
        total_ref[rows_of(chunk)] += jnp.dot(
            dscore.astype(jnp.bfloat16), query, preferred_element_type=jnp.float32
        )


def query_blocks(dims, place, distances, sources, refs):
    tok = dims[0]
    me = place[0]
    key_ref, value_ref, query_ref, grad_ref, score_ref, dprob_ref, total_ref, sem = refs
    copies = []
    for slot, source in enumerate(sources):
        rows = slice(slot * tok, (slot + 1) * tok)
        for target, piece in zip((query_ref, grad_ref), source):
            copies.append(pltpu.make_async_copy(piece, target.at[rows], sem))
    for copy in copies:
        copy.start()
    yield
    for copy in copies:
        copy.wait()

    def block(slot, distance):
        rows = pl.ds(pl.multiple_of(slot * tok, tok), tok)
        index = me ^ distance

        def work(edge):
            head_block(
                dims, place, index, edge, query_ref[rows], grad_ref[rows], key_ref, value_ref,
                score_ref, dprob_ref, total_ref,
            )

        if dims[1]:
            work(False)
            return
        reach = HALF // tok
        edge = (index < HEADS - SKIP - reach) | (index >= reach + SKIP)
        pl.when(edge)(lambda: work(True))
        pl.when(jnp.logical_not(edge))(lambda: work(False))

    @pl.loop(0, 2 * len(distances))
    def _(slot):
        block(slot, 2 * distances[0] + slot)

    yield


def first_kernel(dims, distances, place, *refs):
    tok, halo, _ = dims
    me = place[0]
    query, key, value, grad = refs[:4]
    key_values, refs = refs[4 : 3 + HEADS], refs[3 + HEADS :]
    count = 2 * len(distances) - 1
    others, refs = refs[:count], refs[count:]
    if halo:
        halves, refs = refs[:2], refs[2:]
    total_ref, key_ref, value_ref, query_ref, grad_ref, score_ref, dprob_ref, sem = refs
    mine = pl.ds(pl.multiple_of(me * HEAD_DIM, HEAD_DIM), HEAD_DIM)
    copies = []
    for distance in range(HEADS):
        rows = pl.ds(pl.multiple_of((me ^ distance) * tok + halo, tok), tok)
        pair = (key, value)
        if distance:
            pair = [key_values[distance - 1].at[index] for index in range(2)]
        else:
            pair = (key.at[:, mine], value.at[:, mine])
        for source, target in zip(pair, (key_ref, value_ref)):
            copies.append(pltpu.make_async_copy(source, target.at[rows], sem))
    if halo:
        for side, start in ((0, 0), (1, halo + HEADS * tok)):
            for index, target in enumerate((key_ref, value_ref)):
                copies.append(
                    pltpu.make_async_copy(
                        halves[side].at[index], target.at[pl.ds(start, halo)], sem
                    )
                )
    for copy in copies:
        copy.start()
    sources = [(query.at[:, mine], grad.at[:, mine])]
    sources += [(other.at[0], other.at[1]) for other in others]
    steps = query_blocks(
        dims, place, distances, sources,
        (key_ref, value_ref, query_ref, grad_ref, score_ref, dprob_ref, total_ref, sem),
    )
    next(steps)
    total_ref[...] = jnp.zeros_like(total_ref)
    for copy in copies:
        copy.wait()
    next(steps)


def later_kernel(dims, distances, last, place, before_ref, key_ref, value_ref, *refs):
    tok, halo, _ = dims
    count = 2 * len(distances)
    others, refs = refs[:count], refs[count:]
    split = last and not halo
    if split:
        outs, refs = refs[: HEADS // 2], refs[HEADS // 2 :]
        total_ref, refs = refs[0], refs[1:]
    else:
        total_ref, refs = refs[0], refs[1:]
    sources = [(other.at[0], other.at[1]) for other in others]
    query_ref, grad_ref, score_ref, dprob_ref, sem = refs
    steps = query_blocks(
        dims, place, distances, sources,
        (key_ref, value_ref, query_ref, grad_ref, score_ref, dprob_ref, total_ref, sem),
    )
    next(steps)
    total_ref[...] = before_ref[...]
    next(steps)
    inverse_root = 1.0 / math.sqrt(HEAD_DIM)
    if split:
        pair = 2 * tok
        for distance, out in zip(slot_distances(place[0] // 2, place[2]), outs):
            start = pl.multiple_of(((place[0] // 2) ^ distance) * pair, pair)
            out[...] = (total_ref[pl.ds(start, pair)] * inverse_root).astype(jnp.bfloat16)
    elif last:
        total_ref[...] = total_ref[...] * inverse_root


def head_grads(place, arrays, key_values, query_grads, halves, groups):
    tok = arrays[0].shape[0]
    halo = HALF if halves else 0
    dims = (tok, halo, groups)
    span = HEADS * tok + 2 * halo
    window = min(span, tok + 2 * HALF)
    any_spec = pl.BlockSpec(memory_space=pltpu.HBM)
    vmem = pl.BlockSpec(memory_space=pltpu.VMEM)
    smem = pl.BlockSpec(memory_space=pltpu.SMEM)
    total = jax.ShapeDtypeStruct((span, HEAD_DIM), jnp.float32)
    low = jax.ShapeDtypeStruct((span, HEAD_DIM), jnp.bfloat16)
    piece = jax.ShapeDtypeStruct((2 * tok, HEAD_DIM), jnp.bfloat16)
    params = pltpu.CompilerParams(vmem_limit_bytes=(14 if halo else 10) * 2**20)

    def scratch(pairs):
        return [
            pltpu.VMEM((2 * pairs * tok, HEAD_DIM), jnp.bfloat16),
            pltpu.VMEM((2 * pairs * tok, HEAD_DIM), jnp.bfloat16),
            pltpu.VMEM((window, tok), jnp.float32),
            pltpu.VMEM((window, tok), jnp.float32),
        ]

    def cost(pairs):
        return pl.CostEstimate(
            flops=100 * pairs * tok * window * HEAD_DIM,
            bytes_accessed=8 * span * HEAD_DIM,
            transcendentals=2 * pairs * tok * window,
        )

    sem = [pltpu.SemaphoreType.DMA]
    state = pl.pallas_call(
        functools.partial(first_kernel, dims, (0, 1)),
        out_shape=[total, low, low],
        in_specs=[smem] + [any_spec] * (4 + HEADS - 1 + 3 + len(halves)),
        out_specs=[vmem] * 3,
        scratch_shapes=scratch(2) + sem,
        compiler_params=params,
        cost_estimate=cost(2),
        name="head_first",
    )(place, *arrays, *key_values, *query_grads[:3], *halves)
    for distance in (2, 3):
        last = distance == 3
        split = last and not halo
        others = query_grads[2 * distance - 1 : 2 * distance + 1]
        out = pl.pallas_call(
            functools.partial(later_kernel, dims, (distance,), last),
            out_shape=[piece] * (HEADS // 2) if split else [total],
            in_specs=[smem] + [vmem] * 3 + [any_spec] * 2,
            out_specs=[vmem] * (HEADS // 2 if split else 1),
            scratch_shapes=([pltpu.VMEM(total.shape, total.dtype)] if split else [])
            + scratch(1)
            + sem,
            compiler_params=params,
            cost_estimate=cost(1),
            name="head_later",
        )(place, *state, *others)
        state = [out[0], *state[1:]]
    return out if split else out[0]


def weight_kernel(targets, place, input_ref, *refs):
    pieces, out_refs, grad_ref = refs[:4], refs[4:-1], refs[-1]
    column = place[0] // 2
    tokens = pieces[0].shape[0]
    for slot, piece in enumerate(pieces):
        document = (column % 2) ^ int(slot in (1, 2))
        side = ((column // 2) % 2) ^ int(slot < 2)
        rows = pl.ds(pl.multiple_of(document * tokens, tokens), tokens)
        grad_ref[rows, pl.ds(pl.multiple_of(side * HEAD_DIM, HEAD_DIM), HEAD_DIM)] = piece[...]
    for target, out_ref in zip(targets, out_refs):
        product = jnp.dot(
            input_ref[target], grad_ref[...], preferred_element_type=jnp.float32
        )
        out_ref[...] = product.astype(out_ref.dtype)


def weight_parts(place, inputs, pieces, targets, dtypes):
    _, share, depth = inputs.shape
    width = 2 * HEAD_DIM
    vmem = pl.BlockSpec(memory_space=pltpu.VMEM)
    return pl.pallas_call(
        functools.partial(weight_kernel, targets),
        out_shape=[jax.ShapeDtypeStruct((share, width), dtype) for dtype in dtypes],
        in_specs=[pl.BlockSpec(memory_space=pltpu.SMEM)] + [vmem] * (1 + len(pieces)),
        out_specs=[vmem] * len(targets),
        scratch_shapes=[pltpu.VMEM((depth, width), jnp.bfloat16)],
        compiler_params=pltpu.CompilerParams(vmem_limit_bytes=8 * 2**20),
        cost_estimate=pl.CostEstimate(
            flops=2 * len(targets) * share * depth * width,
            bytes_accessed=2 * depth * (width + len(targets) * share),
            transcendentals=0,
        ),
        name="weight_parts",
    )(place, inputs, *pieces)


def sum_kernel(place, *refs):
    keep_ref, give_ref = refs[-2:]
    share = keep_ref.shape[0]
    for out_ref, core in ((give_ref, 1 - place[2]), (keep_ref, place[2])):
        rows = pl.ds(pl.multiple_of(core * share, share), share)
        total = refs[0][rows]
        for part in refs[1:-2]:
            total = total + part[rows].astype(jnp.float32)
        out_ref[...] = total


def summed(place, parts):
    share, width = parts[0].shape
    vmem = pl.BlockSpec(memory_space=pltpu.VMEM)
    return pl.pallas_call(
        sum_kernel,
        out_shape=[jax.ShapeDtypeStruct((share // 2, width), jnp.float32)] * 2,
        in_specs=[pl.BlockSpec(memory_space=pltpu.SMEM)] + [vmem] * len(parts),
        out_specs=[vmem] * 2,
        compiler_params=pltpu.CompilerParams(vmem_limit_bytes=4 * 2**20),
        name="summed",
    )(place, *parts)


def place_kernel(side, place, *refs):
    parts, out_ref, sem = refs[:2], refs[-2], refs[-1]
    parity = (place[0] % 2) ^ side
    copies = []
    for index, ref in enumerate(parts):
        for column in range(HEADS // 4):
            block = 4 * column + 2 * (place[2] ^ index) + parity
            start = pl.multiple_of(block * HEAD_DIM, HEAD_DIM)
            source = ref.at[:, column * HEAD_DIM : (column + 1) * HEAD_DIM]
            target = out_ref.at[:, pl.ds(start, HEAD_DIM)]
            copies.append(pltpu.make_async_copy(source, target, sem))
    for copy in copies:
        copy.start()
    for copy in copies:
        copy.wait()


def placed(place, side, keep, other, before=None):
    share, width = keep.shape
    vmem = pl.BlockSpec(memory_space=pltpu.VMEM)
    hbm = pl.BlockSpec(memory_space=pltpu.HBM)
    rest = [] if before is None else [before]
    return pl.pallas_call(
        functools.partial(place_kernel, side),
        out_shape=jax.ShapeDtypeStruct((share, 4 * width), jnp.float32),
        in_specs=[pl.BlockSpec(memory_space=pltpu.SMEM), vmem, vmem] + [hbm] * len(rest),
        out_specs=hbm,
        scratch_shapes=[pltpu.SemaphoreType.DMA],
        input_output_aliases={3: 0} if rest else {},
        compiler_params=pltpu.CompilerParams(vmem_limit_bytes=2 * 2**20),
        name="placed",
    )(place, keep, other, *rest)


def ordered(first, own, other, axis):
    return jnp.where(first == 0, jnp.stack([own, other], axis), jnp.stack([other, own], axis))


def gathered_inputs(layer_input, me, parity, core, groups):
    tok, width = layer_input.shape
    columns = lax.axis_size("seq") // 2
    share = width // (columns * 4)
    shaped = layer_input.reshape(tok, columns, 2, 2, share)
    keep = lax.dynamic_index_in_dim(shaped, parity, 2, keepdims=False)
    give = lax.dynamic_index_in_dim(shaped, 1 - parity, 2, keepdims=False)
    both = ordered(parity, keep, exchange(give, "seq", 1), 0)
    both = both.reshape(2 * tok, columns, 2 * share)
    full = ordered(core, both, exchange(both, "dp", 1), 0)
    full = full.reshape(4 * tok, columns, 2 * share).transpose(1, 2, 0)
    if groups == 1:
        here = me // 2
        full = jnp.stack(
            [
                lax.dynamic_index_in_dim(full, here ^ distance, 0, keepdims=False)
                for distance in range(columns)
            ]
        )
    return full


def after(*values):
    return lax.optimization_barrier(values)


def local(queries, key_states, value_states, out_grad, layer_input):
    seq_count = lax.axis_size("seq")
    groups = seq_count // HEADS
    tok = queries.shape[1]
    index = lax.axis_index("seq")
    core = lax.axis_index("dp")
    me = index % HEADS
    group = index // HEADS
    parity = index % 2
    place = jnp.stack([me, group, core]).astype(jnp.int32)
    arrays = [array[0] for array in (queries, key_states, value_states, out_grad)]

    def sent(pieces, distances):
        return {d: exchange(pieces[d], "seq", d) for d in distances}

    keys, values = arrays[1:3]
    source = layer_input[0]
    width = source.shape[1]
    every = (6, 7, 4, 5, 2, 3, 1)
    direct = groups == 1 and width == HEADS * 2 * HEAD_DIM
    if direct:
        pieces = split_heads(place, keys, values, every)
        key_values = sent(pieces, (6, 7, 1, 2, 3))
        for first, second in ((6, 4), (7, 5)):
            key_values[first], pieces[second] = after(key_values[first], pieces[second])
        key_values |= sent(pieces, (4, 5))
        key_values[1], source = after(key_values[1], source)
        block = jax.ShapeDtypeStruct((HEADS, tok, HEAD_DIM), source.dtype)
        keep, give = moved(sides_kernel, [block] * 2, place, source)
        received = exchange(give, "seq", 1)
        sides = [keep, exchange(keep, "dp", 1), received, exchange(received, "dp", 1)]
        shape = (HEADS // 2, 2 * HEAD_DIM, 4 * tok)
        turned = jax.ShapeDtypeStruct(shape, source.dtype)
    else:
        key_values = sent(split_heads(place, keys, values, every), every)
        inputs = gathered_inputs(source, me, parity, core, groups)
    pieces = split_heads(place, arrays[0], arrays[3], every)
    for first, second in ((1, 1), (2, 2), (3, 3), (4, 4), (5, 5), (5, 6), (5, 7)):
        key_values[first], pieces[second] = after(key_values[first], pieces[second])
    if direct:
        sides[1], pieces[7] = after(sides[1], pieces[7])
    query_grads = sent(pieces, every)
    if direct:
        inputs = moved(turned_kernel, [turned], place, *sides)[0]
        query_grads[7], inputs = after(query_grads[7], inputs)
    key_values = [key_values[d] for d in range(1, HEADS)]
    query_grads = [query_grads[d] for d in range(1, HEADS)]
    halves = []
    if groups > 1:
        mine = [lax.dynamic_slice_in_dim(a, me * HEAD_DIM, HEAD_DIM, 1) for a in arrays[1:3]]
        by_distance = jnp.stack([jnp.stack(mine), *key_values])
        rows = jnp.stack(
            [
                lax.dynamic_index_in_dim(by_distance, me ^ block, 0, keepdims=False)
                for block in range(HEADS)
            ]
        )
        rows = rows.transpose(1, 0, 2, 3).reshape(2, HEADS * tok, HEAD_DIM)
        ahead = [(source, source + HEADS) for source in range(seq_count - HEADS)]
        back = [(source + HEADS, source) for source in range(seq_count - HEADS)]
        halves = [
            lax.ppermute(rows[:, -HALF:], "seq", ahead),
            lax.ppermute(rows[:, :HALF], "seq", back),
        ]
    grads = head_grads(place, arrays, key_values, query_grads, halves, groups)
    if groups > 1:
        from_after = lax.ppermute(grads[:HALF].astype(jnp.bfloat16), "seq", back)
        from_before = lax.ppermute(grads[-HALF:].astype(jnp.bfloat16), "seq", ahead)
        inner = grads[HALF:-HALF]
        inner = inner.at[-HALF:].add(from_after.astype(jnp.float32))
        inner = inner.at[:HALF].add(from_before.astype(jnp.float32))
        inner = inner.astype(jnp.bfloat16)
        grads = [
            lax.dynamic_slice_in_dim(inner, ((me // 2) ^ distance) * 2 * tok, 2 * tok, 0)
            for distance in slot_distances(me // 2, core)
        ]

    near = [
        lax.ppermute(piece, ("seq", "dp"), slot_route(slot)) for slot, piece in enumerate(grads)
    ]
    far = [exchange(piece, "seq", 1) for piece in near[2:]]
    held = after(near[0], near[1], *near[2:], *far)
    far = list(held[4:])
    far = [exchange(piece, "seq", 1) for piece in held[:2]] + far

    if groups > 1:
        members = [list(range(first, seq_count, 2)) for first in (0, 1)]

        def scattered(pieces):
            targets = range(inputs.shape[0])
            parts = weight_parts(place, inputs, pieces, targets, [jnp.float32] * len(targets))
            rows = lax.psum_scatter(
                jnp.concatenate(parts), "seq", scatter_dimension=0,
                axis_index_groups=members, tiled=True,
            )
            rows = rows.reshape(2, -1, HEADS // 4, HEAD_DIM)
            keep = lax.dynamic_index_in_dim(rows, core, 0, keepdims=False)
            give = lax.dynamic_index_in_dim(rows, 1 - core, 0, keepdims=False)
            return ordered(core, keep, exchange(give, "dp", 1), 2)

        result = ordered(parity, scattered(near), scattered(far), 3)
        return result.reshape(result.shape[0], HEADS * HEAD_DIM)

    def spread(pieces):
        low = jnp.bfloat16
        across = weight_parts(place, inputs, pieces, (3, 2), (low, low))
        held = after(*across, *pieces)
        across, pieces = held[:2], held[2:]
        beside, total = weight_parts(place, inputs, pieces, (1, 0), (low, jnp.float32))
        parts = zip((3, 2, 1), (*across, beside))
        return [total] + [exchange(part, "seq", 2 * distance) for distance, part in parts]

    first = spread(near)
    far, first[1] = after(far, first[1])
    second = spread(far)
    near_keep, near_give = summed(place, first)
    far_keep, far_give = summed(place, second)
    half = placed(place, 0, near_keep, exchange(near_give, "dp", 1))
    return placed(place, 1, far_keep, exchange(far_give, "dp", 1), half)


def solution(mesh):
    spec = P(("parts", "dp"), "seq", None)
    out_specs = P(("parts", "seq", "dp"), None)
    return jax.shard_map(
        local, mesh=mesh, in_specs=(spec,) * 5, out_specs=out_specs, check_vma=False
    )
```
